128 devices in a mesh: dp: 32 (over z, y, core), group: 4 (over x).
Axes of the slice: x: 4, y: 4, z: 4, core: 2. Of those that a mesh axis runs over, the one named last changes fastest.
Arguments:
- hidden_in: bfloat16 [256, 128, 1024], P(('dp', 'group')), may hold values from -6 to 6
- out_grad: bfloat16 [256, 128, 1024], P(('dp', 'group')), may hold values from -6 to 6
- seq_owner: int32 [160], replicated, may hold values from 0 to 127, as said below
- token_place: int32 [256, 128], P(('dp', 'group')), may hold values from 0 to 4603, as said below
- matrix_slot: int32 [7], replicated, may hold values from 0 to 7, as said below
- weight_slots: float32 [8, 1024, 3072], P('group', 'dp'), may hold values from -1 to 1
- momentum_slots: float32 [8, 1024, 3072], P('group', 'dp'), may hold values from -448 to 448
- gains: float32 [2304], replicated, may hold values from 0.8 to 6
- gain_momentum: float32 [2304], replicated, may hold values from -448 to 448
Outputs:
- hidden_out: bfloat16 [256, 128, 1024], P(('dp', 'group'))
- in_grad: float32 [256, 128, 1024], P(('dp', 'group'))
- weight_grad: float32 [8, 1024, 3072], P('group', 'dp')
- momentum_new: float32 [8, 1024, 3072], P('group', 'dp')
- weight_new: float32 [8, 1024, 3072], P('group', 'dp')
- gain_grad: float32 [2304], replicated
- gain_momentum_new: float32 [2304], replicated
- gain_new: float32 [2304], replicated
The draws below stay inside these ranges and needn't reach their ends.
Inputs may be any that keep to these rules, and one draw needn't show every extreme that they name: `seq_owner`: not falling; each replica is named 1 or 2 times, exactly 32 of them 2 times; a replica's sequences fill its first slots. `token_place`: strictly rising along each slot's tokens, by 1 to 4 from one token to the next. `matrix_slot`: seven distinct slots, for the query, key, value, output, gate, up and down projections in this order; slot s belongs to group index s // 2.
All inputs are finite; a program needn't handle non-finite values.
Results may differ from the reference program's by a relative error of at most 0.029.
Values may be sent and summed in bfloat16 or wider, within the bound.
No kernel may reach another device: no remote copies, remote signals or barrier semaphores. Data moves between devices by JAX's collectives and lax.ppermute only.
A program may use at most 320 MiB of HBM per device.

```python
import jax
import jax.numpy as jnp
from jax import lax

D = 1024
HEADS = 16
KV = 8
HD = 128
FF = 3072
SEQ = 128
SLOTS = 2
NS_ITERS = 5
EXTRA = 32
SEQS = 160
N_DP = 32
N_GROUP = 4
DEVICES = 128


def slot_choice(key):
    shuffled = jax.random.permutation(key, 2 * N_GROUP)
    return shuffled[:7].astype(jnp.int32)


def draw_matrix_slot(key, part):
    return slot_choice(key)


def draw_weight_slots(key, part):
    chosen = slot_choice(key)
    key = jax.random.fold_in(key, 2)
    spreads = (D ** (-0.5), D ** (-0.5), D ** (-0.5), 0.09, D ** (-0.5), D ** (-0.5), 0.5 * FF ** (-0.5))
    slot_ids = jnp.arange(2 * N_GROUP, dtype=jnp.int32)
    per_slot = jnp.full((2 * N_GROUP,), D ** (-0.5), jnp.float32)
    for number in range(7):
        per_slot = jnp.where(slot_ids == chosen[number], spreads[number], per_slot)
    full_shape = (2 * N_GROUP, D, FF)
    unit_draw = jax.random.truncated_normal(key, -4.0, 4.0, full_shape, jnp.float32)
    return unit_draw * per_slot[:, None, None]


def draw_gains(key, part):
    key = jax.random.fold_in(key, 3)
    ramp = jnp.arange(D, dtype=jnp.float32) / (D - 1)
    rising = 1.0 + 2.0 * ramp
    jitter = jax.random.uniform(key, (2 * D + 2 * HD,), jnp.float32, 0.85, 1.15)
    base_gain = jnp.concatenate([rising, rising, jnp.ones((2 * HD,), jnp.float32)])
    return base_gain * jitter


def draw_seq_owner(key, part):
    key = jax.random.fold_in(key, 4)
    ranking = jax.random.permutation(key, DEVICES)
    counts = SLOTS - 1 + (ranking < EXTRA).astype(jnp.int32)
    ends = jnp.cumsum(counts)
    places = jnp.arange(SEQS, dtype=jnp.int32)
    return jnp.sum((ends[None, :] <= places[:, None]).astype(jnp.int32), axis=1).astype(jnp.int32)


def draw_token_place(key, part):
    key = jax.random.fold_in(key, 5)
    step_key, first_key, pick_key = jax.random.split(key, 3)
    rows = DEVICES * SLOTS
    strides = jax.random.randint(step_key, (rows, SEQ), 1, 5, jnp.int32)
    first = jax.random.randint(first_key, (rows, 1), 0, 4096, jnp.int32)
    picked = jax.random.permutation(pick_key, rows)[:2].astype(jnp.int32)
    row_ids = jnp.arange(rows, dtype=jnp.int32)[:, None]
    top_row = row_ids == picked[0]
    low_row = row_ids == picked[1]
    strides = jnp.where(top_row, 4, strides).astype(jnp.int32)
    first = jnp.where(top_row, 4095, jnp.where(low_row, 0, first)).astype(jnp.int32)
    return (first + jnp.cumsum(strides, axis=1) - strides[:, :1]).astype(jnp.int32)


def levels(stream_key, shape, cuts, least, high):
    def one(position, shards_of):
        draws = jax.random.uniform(jax.random.fold_in(jax.random.fold_in(stream_key, 6), position), (shards_of,), jnp.float32, least / len(cuts), high / len(cuts))
        return jnp.repeat(jnp.exp(draws), shape[position] // shards_of).reshape((-1,) + (1,) * (len(shape) - position - 1))

    factor_of = one(*cuts[0])
    for cut in cuts[1:]:
        factor_of = factor_of * one(*cut)
    return factor_of


def centred(rng, extent, width, limit, cuts=(), held_as=jnp.bfloat16):
    result = jax.random.normal(rng, extent, jnp.float32) * width
    if len(cuts) > 0:
        result = levels(rng, extent, cuts, -0.22, 0.18) * result
    return jnp.clip(result, min=-limit, max=limit).astype(held_as)


def setup_inputs(seed: int = 0) -> dict:
    key_list = jax.random.split(jax.random.key(seed), 10)
    hidden_in = centred(key_list[0], (DEVICES * SLOTS, SEQ, D), 1.0, 6.0, ((0, 128),))
    out_grad = centred(key_list[1], (DEVICES * SLOTS, SEQ, D), 1.0, 6.0, ((0, 128),))
    seq_owner = draw_seq_owner(jax.random.fold_in(key_list[9], 71), 0)
    token_place = draw_token_place(jax.random.fold_in(key_list[9], 71), 0)
    matrix_slot = draw_matrix_slot(jax.random.fold_in(key_list[9], 71), 0)
    weight_slots = draw_weight_slots(jax.random.fold_in(key_list[9], 71), 0)
    momentum_slots = centred(key_list[6], (2 * N_GROUP, D, FF), (0.5 * (SEQS * SEQ) ** 0.5), 448.0, ((0, 4), (1, 32)), jnp.float32)
    gains = draw_gains(jax.random.fold_in(key_list[9], 71), 0)
    gain_momentum = centred(key_list[8], (2 * D + 2 * HD,), (0.5 * (SEQS * SEQ) ** 0.5), 448.0, (), jnp.float32)
    return {"hidden_in": hidden_in, "out_grad": out_grad, "seq_owner": seq_owner, "token_place": token_place, "matrix_slot": matrix_slot, "weight_slots": weight_slots, "momentum_slots": momentum_slots, "gains": gains, "gain_momentum": gain_momentum}


norm_eps = 1e-06
frob_eps = 1e-07
rope_base = 1000000.0
coef_linear = 3.4445
coef_square = -4.775
coef_quartic = 2.0315
momentum_keep = 0.95
learn_rate = 0.15
weight_decay = 0.1
gain_rate = 0.5
masked_score = -1e+30

@jax.custom_vjp
def low(v):
    return lax.optimization_barrier(v.astype(jnp.bfloat16)).astype(jnp.float32)

@jax.custom_vjp
def low_back(v):
    return v

def low_keep(v):
    return (low(v), None)

def low_pass(kept, grad):
    return (grad,)

def back_keep(v):
    return (v, None)

def back_low(kept, grad):
    return (low(grad),)
low.defvjp(low_keep, low_pass)
low_back.defvjp(back_keep, back_low)

def rope_tables(places_int, head_width):
    half_width = head_width // 2
    exponent = jnp.arange(half_width, dtype=jnp.float32) * (-2.0 / head_width)
    inverse = jnp.power(rope_base, exponent)
    places = places_int.astype(jnp.float32)
    angles = places[:, :, None] * inverse[None, None, :]
    return (jnp.cos(angles)[:, :, None, :], jnp.sin(angles)[:, :, None, :])

def rotate(values, cosine, sine_part):
    half_width = values.shape[-1] // 2
    leading = values[..., :half_width]
    trailing = values[..., half_width:]
    return jnp.concatenate([leading * cosine - trailing * sine_part, trailing * cosine + leading * sine_part], axis=-1)

def matmul(left, right):
    return jnp.dot(left, right, precision=lax.Precision.HIGHEST, preferred_element_type=jnp.float32)

def head_normalize(raw_proj, slot_count, length, heads, gain):
    shaped = raw_proj.reshape(slot_count, length, heads, HD)
    scale = lax.rsqrt(lax.optimization_barrier(jnp.mean(shaped * shaped, axis=-1, keepdims=True)) + norm_eps)
    return shaped * scale * gain

def block(mats, gains, tokens, cosine, sine_part):
    w_query, w_key, w_value, w_output, w_gate, w_up, w_down = mats
    slot_count = tokens.shape[0]
    length = tokens.shape[1]
    flat_rows = tokens.reshape(slot_count * length, D)
    gain_one = gains[:D]
    gain_two = gains[D:2 * D]
    gain_query = gains[2 * D:2 * D + HD]
    gain_key = gains[2 * D + HD:]
    scale_one = lax.rsqrt(lax.optimization_barrier(jnp.mean(flat_rows * flat_rows, axis=-1, keepdims=True)) + norm_eps)
    input_one = low(flat_rows * scale_one * gain_one)
    query_raw = low_back(matmul(input_one, w_query))
    key_raw = low_back(matmul(input_one, w_key))
    value_heads = low(low_back(matmul(input_one, w_value))).reshape(slot_count, length, KV, HD)
    query_low = low(rotate(head_normalize(query_raw, slot_count, length, HEADS, gain_query), cosine, sine_part))
    key_low = low(rotate(head_normalize(key_raw, slot_count, length, KV, gain_key), cosine, sine_part))
    query_group = query_low.reshape(slot_count, length, KV, HEADS // KV, HD)
    causal = jnp.arange(length)[:, None] >= jnp.arange(length)[None, :]
    raw_scores = jnp.einsum('bikgw,bjkw->bkgij', query_group, key_low, precision=lax.Precision.HIGHEST)
    scores = jnp.where(causal, low_back(raw_scores * HD ** (-0.5)), masked_score)
    row_top = lax.optimization_barrier(jnp.max(scores, axis=-1, keepdims=True))
    exponent_terms = jnp.exp(scores - row_top)
    probs = low(exponent_terms / lax.optimization_barrier(jnp.sum(exponent_terms, axis=-1, keepdims=True)))
    attended = jnp.einsum('bkgij,bjkw->bikgw', probs, value_heads, precision=lax.Precision.HIGHEST)
    attn_in = low(low_back(attended.reshape(slot_count * length, HEADS * HD)))
    residual = flat_rows + low_back(matmul(attn_in, w_output))
    scale_two = lax.rsqrt(lax.optimization_barrier(jnp.mean(residual * residual, axis=-1, keepdims=True)) + norm_eps)
    input_two = low(residual * scale_two * gain_two)
    gate_proj = low_back(matmul(input_two, w_gate))
    up_proj = low_back(matmul(input_two, w_up))
    act_in = low(jax.nn.silu(gate_proj) * up_proj)
    return (residual + matmul(act_in, w_down)).reshape(slot_count, length, D)

def reference(hidden_in, out_grad, seq_owner, token_place, matrix_slot, weight_slots, momentum_slots, gains, gain_momentum):
    devices = N_DP * N_GROUP
    slot_total = 2 * N_GROUP
    widths = (HEADS * HD, KV * HD, KV * HD, HEADS * HD, FF, FF, FF)
    rounded = low(weight_slots)
    jobs = [lax.dynamic_index_in_dim(rounded, matrix_slot[number].astype(jnp.int32), 0, keepdims=False)[:, :widths[number]] for number in range(7)]
    mats = (jobs[0], jobs[1], jobs[2], jobs[3].T, jobs[4], jobs[5], jobs[6].T)
    replicas = jnp.arange(devices, dtype=jnp.int32)
    counts = lax.optimization_barrier(jnp.sum((seq_owner[None, :] == replicas[:, None]).astype(jnp.int32), axis=1))
    tokens_all = hidden_in.astype(jnp.float32).reshape(devices, SLOTS, SEQ, D)
    cotan_all = out_grad.astype(jnp.float32).reshape(devices, SLOTS, SEQ, D)
    places_all = token_place.reshape(devices, SLOTS, SEQ)

    def one_replica(carried, inputs):
        tokens, cotangent, places, live_count = inputs
        live_mask = (jnp.arange(SLOTS, dtype=jnp.int32) < live_count).astype(jnp.float32)[:, None, None]
        cosine, sine_part = rope_tables(places, HD)

        def masked_block(mats_in, gains_in, tokens_in):
            return block(mats_in, gains_in, tokens_in, cosine, sine_part) * live_mask
        output, pullback = jax.vjp(masked_block, mats, gains, tokens)
        mat_grads, gain_grads, token_grads = pullback(cotangent * live_mask)
        job_grads = (mat_grads[0], mat_grads[1], mat_grads[2], mat_grads[3].T, mat_grads[4], mat_grads[5], mat_grads[6].T)
        summed, gain_running = carried
        summed = tuple((running + low(fresh_grad) for running, fresh_grad in zip(summed, job_grads)))
        return ((summed, gain_running + low(gain_grads)), (output.astype(jnp.bfloat16), token_grads))
    start_carry = (tuple((jnp.zeros((D, width_value), jnp.float32) for width_value in widths)), jnp.zeros(gains.shape, jnp.float32))
    final_carry, stacked = lax.scan(one_replica, start_carry, (tokens_all, cotan_all, places_all, counts))
    summed, gain_grad = final_carry
    hidden_out = stacked[0].reshape(devices * SLOTS, SEQ, D)
    in_grad = stacked[1].reshape(devices * SLOTS, SEQ, D)
    slot_ids = jnp.arange(slot_total, dtype=jnp.int32)
    weight_grad = jnp.zeros((slot_total, D, FF), jnp.float32)
    slot_width = jnp.zeros((slot_total,), jnp.int32)
    for number in range(7):
        padded = jnp.pad(summed[number], ((0, 0), (0, FF - widths[number])))
        matches = slot_ids == matrix_slot[number]
        weight_grad = weight_grad + jnp.where(matches[:, None, None], padded[None], 0.0)
        slot_width = slot_width + jnp.where(matches, widths[number], 0).astype(jnp.int32)
    column_mask = (jnp.arange(FF, dtype=jnp.int32)[None, :] < slot_width[:, None]).astype(jnp.float32)[:, None, :]
    momentum_new = column_mask * (momentum_keep * momentum_slots + weight_grad)
    direction = weight_grad + momentum_keep * momentum_new
    norms = jnp.sqrt(lax.optimization_barrier(jnp.sum(direction * direction, axis=(1, 2))))
    iterate = low(direction / (norms[:, None, None] + frob_eps))
    for sweep_index in range(NS_ITERS):
        gram = low(jnp.einsum('sin,sjn->sij', iterate, iterate, precision=lax.Precision.HIGHEST))
        gram_square = jnp.einsum('sij,sjk->sik', gram, gram, precision=lax.Precision.HIGHEST)
        poly = low(coef_square * gram + coef_quartic * gram_square)
        iterate = low(coef_linear * iterate + jnp.einsum('sij,sjn->sin', poly, iterate, precision=lax.Precision.HIGHEST))
    update_scale = 0.2 * jnp.sqrt(jnp.maximum(slot_width, D).astype(jnp.float32))
    weight_new = column_mask * (weight_slots * (1.0 - learn_rate * weight_decay) - learn_rate * update_scale[:, None, None] * iterate)
    gain_momentum_new = momentum_keep * gain_momentum + gain_grad
    gain_step = gain_grad + momentum_keep * gain_momentum_new
    bounds = (0, D, 2 * D, 2 * D + HD, 2 * D + 2 * HD)
    scaled_parts = []
    for number in range(4):
        segment = gain_step[bounds[number]:bounds[number + 1]]
        scaled_parts.append(segment * lax.rsqrt(jnp.mean(segment * segment) + norm_eps))
    gain_new = gains - gain_rate * jnp.concatenate(scaled_parts)
    return (hidden_out, in_grad, weight_grad, momentum_new, weight_new, gain_grad, gain_momentum_new, gain_new)
```

```python
import functools

import jax
import jax.numpy as jnp
from jax import lax
from jax.experimental import pallas as pl
from jax.experimental.pallas import tpu as pltpu
from jax.sharding import Mesh
from jax.sharding import PartitionSpec as P

D = 1024
HEADS = 16
KV = 8
HD = 128
FF = 3072
SEQ = 128
NS_ITERS = 5
WIDTHS = (HEADS * HD, KV * HD, KV * HD, HEADS * HD, FF, FF, FF)
DP_GROUP = ("dp_0", "dp_1", "dp_2", "group")
LOW = jnp.bfloat16
F32 = jnp.float32

norm_eps = 1e-06
frob_eps = 1e-07
rope_base = 1000000.0
coef_linear = 3.4445
coef_square = -4.775
coef_quartic = 2.0315
momentum_keep = 0.95
learn_rate = 0.15
weight_decay = 0.1
gain_rate = 0.5
masked_score = -1e30
score_scale = HD ** (-0.5)

NEAR = ((0, 1), (1, 0), (2, 3), (3, 2))
FAR = ((0, 3), (3, 0), (1, 2), (2, 1))
LINKS = (("dp_0", NEAR), ("dp_1", NEAR), ("dp_0", FAR), ("dp_1", FAR))
MASKS = (0, 3, 1, 2)


def place_of(mask):
    return jnp.where(mask == 0, 0, jnp.where(mask == 3, 1, mask + 1))


def swap(x):
    return lax.ppermute(x, "dp_2", ((0, 1), (1, 0)))


def together(arrays):
    return list(lax.optimization_barrier(tuple(arrays)))


def gather_steps(quarters, step):
    fresh = []
    for i in range(4):
        axis, pairs = LINKS[(step + i) % 4]
        fresh.append(lax.ppermute(quarters[i], axis, pairs))
    return [
        jnp.concatenate([quarters[i], fresh[i]], axis=(step + i) % 4) for i in range(4)
    ]


def gather_quarters(quarters):
    rows = quarters[0].shape[0]
    held = [q.reshape(1, 1, 1, 1, rows, q.shape[1]) for q in quarters]
    for step in range(4):
        held = gather_steps(held, step)
        if step < 3:
            held = together(held)
    return [q.reshape(16 * rows, q.shape[-1]) for q in held]


def scatter_quarters(quarters):
    rows = quarters[0].shape[0] // 16
    held = [q.reshape(2, 2, 2, 2, rows, q.shape[1]) for q in quarters]
    for step in range(4):
        sent = [lax.slice_in_dim(held[i], 1, 2, axis=(step + i) % 4) for i in range(4)]
        kept = [lax.slice_in_dim(held[i], 0, 1, axis=(step + i) % 4) for i in range(4)]
        got = []
        for i in range(4):
            axis, pairs = LINKS[(step + i) % 4]
            got.append(lax.ppermute(sent[i], axis, pairs))
        held = [(kept[i].astype(F32) + got[i].astype(F32)).astype(LOW) for i in range(4)]
        if step < 3:
            held = together(held)
    return [q.reshape(rows, q.shape[-1]) for q in held]


def gather_group(halves):
    held = [h[None, None] for h in halves]
    for step in range(2):
        fresh = [lax.ppermute(held[i], "group", (NEAR, FAR)[(step + i) % 2]) for i in range(2)]
        held = [jnp.concatenate([held[i], fresh[i]], axis=(step + i) % 2) for i in range(2)]
    return [h.reshape(8, *h.shape[3:]) for h in held]


def scatter_group(halves):
    held = [h.reshape(2, 2, 2, *h.shape[1:]) for h in halves]
    for step in range(2):
        fresh = []
        for i in range(2):
            axis = (step + i) % 2
            sent = lax.slice_in_dim(held[i], 1, 2, axis=axis)
            kept = lax.slice_in_dim(held[i], 0, 1, axis=axis)
            got = lax.ppermute(sent, "group", (NEAR, FAR)[axis])
            total = kept.astype(F32) + got.astype(F32)
            fresh.append(total.astype(LOW) if step == 0 else total)
        held = fresh
    return [h.reshape(h.shape[2:]) for h in held]


def sum_everywhere(x):
    steps = [("dp_2", ((0, 1), (1, 0))), *LINKS, ("group", NEAR), ("group", FAR)]
    for axis, pairs in steps:
        x = x + lax.ppermute(x, axis, pairs)
    return x


def dot(left, right, dims=((1,), (0,))):
    return lax.dot_general(left, right, (dims, ((), ())), preferred_element_type=F32)


ROWS = ((0,), (0,))
LAST = ((1,), (1,))
PLAIN = ((1,), (0,))


def split_two(x):
    high = lax.reduce_precision(x, exponent_bits=8, mantissa_bits=7)
    return high.astype(LOW), (x - high).astype(LOW)


def in_two(left, right):
    rows = left.shape[0]
    both_parts = dot(jnp.concatenate(split_two(left), axis=0), right)
    return both_parts[:rows] + both_parts[rows:]


def half_turn(u):
    return jnp.concatenate([u[:, HD // 2 :], u[:, : HD // 2]], axis=1)


def head_forward(raw, gain, cosine, sine):
    scale = lax.rsqrt(jnp.mean(raw * raw, axis=-1, keepdims=True) + norm_eps)
    normed = raw * scale
    gained = normed * gain
    turned = gained * cosine + half_turn(gained) * sine
    return normed, scale, turned.astype(LOW)


def softmax_parts(query, key):
    scores = dot(query, key, LAST) * score_scale
    rows = lax.broadcasted_iota(jnp.int32, scores.shape, 0)
    columns = lax.broadcasted_iota(jnp.int32, scores.shape, 1)
    scores = jnp.where(rows >= columns, scores, masked_score)
    terms = jnp.exp(scores - jnp.max(scores, axis=-1, keepdims=True))
    return terms / jnp.sum(terms, axis=-1, keepdims=True)


def attend_kernel(raw_ref, cos_ref, sin_ref, gain_ref, out_ref):
    cosine, sine = cos_ref[...], sin_ref[...]
    _, _, key = head_forward(raw_ref[:, 2 * HD : 3 * HD], gain_ref[1:2, :], cosine, sine)
    value = raw_ref[:, 3 * HD :].astype(LOW)
    for h in range(2):
        at = slice(h * HD, (h + 1) * HD)
        _, _, query = head_forward(raw_ref[:, at], gain_ref[0:1, :], cosine, sine)
        probs = softmax_parts(query, key).astype(LOW)
        out_ref[:, at] = dot(probs, value).astype(LOW)


def head_backward(grad, normed, scale, gain, cosine, sine):
    back = grad * cosine - half_turn(grad) * sine
    term = jnp.sum(back * normed, axis=0, keepdims=True)
    g = back * gain
    raw = scale * (g - normed * jnp.mean(g * normed, axis=-1, keepdims=True))
    return raw.astype(LOW), term


def attend_back_kernel(raw_ref, grad_ref, cos_ref, sin_ref, gain_ref, out_ref, term_ref):
    cosine, sine = cos_ref[...], sin_ref[...]
    key_hat, key_scale, key = head_forward(
        raw_ref[:, 2 * HD : 3 * HD], gain_ref[1:2, :], cosine, sine
    )
    value = raw_ref[:, 3 * HD :].astype(LOW)
    grad_value = jnp.zeros((SEQ, HD), F32)
    grad_key = jnp.zeros((SEQ, HD), F32)
    query_term = jnp.zeros((1, HD), F32)
    for h in range(2):
        at = slice(h * HD, (h + 1) * HD)
        query_hat, query_scale, query = head_forward(
            raw_ref[:, at], gain_ref[0:1, :], cosine, sine
        )
        probs = softmax_parts(query, key)
        grad_attn = grad_ref[:, at]
        grad_value = grad_value + dot(probs.astype(LOW), grad_attn, ROWS)
        grad_probs = dot(grad_attn, value, LAST)
        inner = jnp.sum(probs * grad_probs, axis=-1, keepdims=True)
        grad_scores = (probs * (grad_probs - inner)).astype(LOW)
        grad_query = dot(grad_scores, key) * score_scale
        grad_key = grad_key + dot(grad_scores, query, ROWS) * score_scale
        raw, term = head_backward(
            grad_query, query_hat, query_scale, gain_ref[0:1, :], cosine, sine
        )
        out_ref[:, at] = raw
        query_term = query_term + term
    raw, key_term = head_backward(grad_key, key_hat, key_scale, gain_ref[1:2, :], cosine, sine)
    out_ref[:, 2 * HD : 3 * HD] = raw
    out_ref[:, 3 * HD :] = grad_value.astype(LOW)
    spare = jnp.zeros((6, HD), F32)
    term_ref[...] = jnp.concatenate([query_term, key_term, spare], axis=0)


def by_sequence(width):
    return pl.BlockSpec((SEQ, width), lambda s: (s, 0))


def whole(rows, width):
    return pl.BlockSpec((rows, width), lambda s: (0, 0))


def attend(raw, cosine, sine, gain_rows):
    tokens = raw.shape[0]
    return pl.pallas_call(
        attend_kernel,
        grid=(tokens // SEQ,),
        in_specs=[by_sequence(4 * HD), by_sequence(HD), by_sequence(HD), whole(8, HD)],
        out_specs=by_sequence(2 * HD),
        out_shape=jax.ShapeDtypeStruct((tokens, 2 * HD), LOW),
        cost_estimate=pl.CostEstimate(
            flops=tokens * SEQ * HD * 8, bytes_accessed=tokens * HD * 32, transcendentals=tokens * 256
        ),
    )(raw, cosine, sine, gain_rows)


def attend_back(raw, grad_attn, cosine, sine, gain_rows):
    tokens = raw.shape[0]
    grad_raw, terms = pl.pallas_call(
        attend_back_kernel,
        grid=(tokens // SEQ,),
        in_specs=[
            by_sequence(4 * HD),
            by_sequence(2 * HD),
            by_sequence(HD),
            by_sequence(HD),
            whole(8, HD),
        ],
        out_specs=[by_sequence(4 * HD), pl.BlockSpec((8, HD), lambda s: (s, 0))],
        out_shape=[
            jax.ShapeDtypeStruct((tokens, 4 * HD), LOW),
            jax.ShapeDtypeStruct((tokens // SEQ * 8, HD), F32),
        ],
        cost_estimate=pl.CostEstimate(
            flops=tokens * SEQ * HD * 24, bytes_accessed=tokens * HD * 40, transcendentals=tokens * 256
        ),
    )(raw, grad_attn, cosine, sine, gain_rows)
    return grad_raw, jnp.sum(terms.reshape(-1, 8, HD), axis=0)


def shared_sum(partial):
    own = partial.shape[0] // 2
    return partial[:own] + swap(partial[own:].astype(LOW)).astype(F32)


def both(x):
    return jnp.concatenate([x, swap(x)], axis=0)


def norm_back(grad_hat, normed, scale):
    return scale * (grad_hat - normed * jnp.mean(grad_hat * normed, axis=-1, keepdims=True))


def cut(x, core, i, width):
    start = (core * 4 + i) * width
    return x[:, start : start + width]


def shards(
    hidden_in,
    out_grad,
    seq_owner,
    token_place,
    matrix_slot,
    weight_slots,
    momentum_slots,
    gains,
    gain_momentum,
):
    slot_count, length = hidden_in.shape[:2]
    tok_count = slot_count * length
    z, y = lax.axis_index("dp_0"), lax.axis_index("dp_1")
    core, group = lax.axis_index("dp_2"), lax.axis_index("group")
    first_core = core == 0
    replica = ((z * 4 + y) * 2 + core) * 4 + group

    def core_pick(zero, one):
        return jnp.where(first_core, zero, one)

    weight_low = weight_slots.astype(LOW)
    slots_top, slots_low = gather_group([weight_low[:, :16], weight_low[:, 16:]])
    projections = []
    for m in range(7):
        slot = matrix_slot[m]
        at = place_of(jnp.bitwise_xor(group, slot // 2)) * 2 + slot % 2
        rows = [
            lax.dynamic_index_in_dim(part, at, 0, keepdims=False)[:, : WIDTHS[m]]
            for part in (slots_top, slots_low)
        ]
        projections.append(jnp.concatenate(rows, axis=0))
    heads_by_core, inner_by_core = [], []
    for c in range(2):
        heads, inner = [], []
        for i in range(4):
            heads += [
                cut(projections[0], c, i, 2 * HD),
                cut(projections[1], c, i, HD),
                cut(projections[2], c, i, HD),
                cut(projections[3], c, i, 2 * HD),
            ]
            inner += [cut(projections[m], c, i, FF // 8) for m in (4, 5, 6)]
        heads_by_core.append(jnp.concatenate(heads, axis=1))
        inner_by_core.append(jnp.concatenate(inner, axis=1))

    def chip_rows(by_core):
        mine = core_pick(by_core[0], by_core[1])
        got = swap(core_pick(by_core[1], by_core[0]))
        return core_pick(
            jnp.concatenate([mine, got], axis=0), jnp.concatenate([got, mine], axis=0)
        )

    heads_rows = chip_rows(heads_by_core)
    inner_rows = chip_rows(inner_by_core)
    HW, IW = 6 * HD, 3 * FF // 8
    w_heads = gather_quarters([heads_rows[:, i * HW : (i + 1) * HW] for i in range(4)])
    w_inner = gather_quarters([inner_rows[:, i * IW : (i + 1) * IW] for i in range(4)])
    w_raw = [w[:, : 4 * HD] for w in w_heads]
    w_out = [w[:, 4 * HD :] for w in w_heads]
    w_gate_up = [w[:, : FF // 4] for w in w_inner]
    w_down = [w[:, FF // 4 :] for w in w_inner]

    column = lax.broadcasted_iota(jnp.int32, (D, D), 1)
    source = lax.broadcasted_iota(jnp.int32, (D, D), 0)
    block = column // 64
    near_z, near_y = block // 8, (block // 4) % 2
    far_z, far_y = (block // 2) % 2, block % 2
    from_z = jnp.bitwise_xor(z, jnp.bitwise_xor(near_z, far_z * 3))
    from_y = jnp.bitwise_xor(y, jnp.bitwise_xor(near_y, far_y * 3))
    reorder = (source == (from_z * 4 + from_y) * 64 + column % 64).astype(LOW)

    live_count = jnp.sum((seq_owner == replica).astype(jnp.int32))
    live_slot = (jnp.arange(slot_count, dtype=jnp.int32) < live_count).astype(F32)
    live_token = jnp.repeat(live_slot, length)[:, None]
    tokens = dot(hidden_in.reshape(tok_count, D), reorder)
    grad_out = dot(out_grad.reshape(tok_count, D), reorder) * live_token
    grad_low = both(grad_out.astype(LOW))
    layer_gains = jnp.dot(
        gains[: 2 * D].reshape(2, D), reorder.astype(F32), precision=lax.Precision.HIGHEST
    )
    gain_one, gain_two = layer_gains[0:1], layer_gains[1:2]
    gain_rows = jnp.pad(gains[2 * D :].reshape(2, HD), ((0, 6), (0, 0)))
    places = both(token_place).astype(F32).reshape(-1, 1)
    exponent = jnp.arange(HD // 2, dtype=F32) * (-2.0 / HD)
    angles = places * jnp.power(rope_base, exponent)[None, :]
    cosine, sine = jnp.cos(angles), jnp.sin(angles)
    cosine = jnp.concatenate([cosine, cosine], axis=1)
    sine = jnp.concatenate([-sine, sine], axis=1)

    scale_one = lax.rsqrt(jnp.mean(tokens * tokens, axis=-1, keepdims=True) + norm_eps)
    normed_one = tokens * scale_one
    input_one = both((normed_one * gain_one).astype(LOW))
    raw = [dot(input_one, w) for w in w_raw]
    attn = [attend(r, cosine, sine, gain_rows) for r in raw]
    branch = sum(dot(a, w, LAST) for a, w in zip(attn, w_out))
    residual = tokens + shared_sum(branch)
    scale_two = lax.rsqrt(jnp.mean(residual * residual, axis=-1, keepdims=True) + norm_eps)
    normed_two = residual * scale_two
    input_two = both((normed_two * gain_two).astype(LOW))
    act, grad_inner, grad_two = [], [], 0.0
    outward = 0.0
    for i in range(4):
        gate_up = dot(input_two, w_gate_up[i])
        gate, up = gate_up[:, : FF // 8], gate_up[:, FF // 8 :]
        sigmoid = jax.nn.sigmoid(gate)
        swish = gate * sigmoid
        act.append((swish * up).astype(LOW))
        grad_act = dot(grad_low, w_down[i])
        slope = sigmoid * (1.0 + gate * (1.0 - sigmoid))
        grad_inner.append(
            jnp.concatenate(
                [(grad_act * up * slope).astype(LOW), (grad_act * swish).astype(LOW)], axis=1
            )
        )
        outward = outward + dot(act[i], w_down[i], LAST)
        grad_two = grad_two + dot(grad_inner[i], w_gate_up[i], LAST)
    result = (residual + shared_sum(outward)) * live_token
    hidden_out = dot(result.astype(LOW), reorder, LAST).astype(LOW)

    inner_terms = [
        jnp.concatenate(
            [
                dot(input_two, grad_inner[i], ROWS).astype(LOW),
                dot(grad_low, act[i], ROWS).astype(LOW),
            ],
            axis=1,
        )
        for i in range(4)
    ]
    inner_sums = scatter_quarters(inner_terms)
    grad_two = shared_sum(grad_two)
    gain_two_term = jnp.sum(grad_two * normed_two, axis=0, keepdims=True)
    grad_residual = grad_out + norm_back(grad_two * gain_two, normed_two, scale_two)
    branch_low = both(grad_residual.astype(LOW))
    grad_one, head_terms, grad_raw = 0.0, 0.0, []
    for i in range(4):
        grad_attn = dot(branch_low, w_out[i]).astype(LOW)
        fresh, term = attend_back(raw[i], grad_attn, cosine, sine, gain_rows)
        grad_raw.append(fresh)
        head_terms = head_terms + term
        grad_one = grad_one + dot(fresh, w_raw[i], LAST)
    heads_terms = [
        jnp.concatenate(
            [
                dot(input_one, grad_raw[i], ROWS).astype(LOW),
                dot(branch_low, attn[i], ROWS).astype(LOW),
            ],
            axis=1,
        )
        for i in range(4)
    ]
    heads_sums = scatter_quarters(heads_terms)
    grad_one = shared_sum(grad_one)
    gain_one_term = jnp.sum(grad_one * normed_one, axis=0, keepdims=True)
    in_grad = grad_residual + norm_back(grad_one * gain_one, normed_one, scale_one)
    in_high, in_low = split_two(in_grad)
    in_grad = dot(in_high, reorder, LAST) + dot(in_low, reorder, LAST)
    layer_terms = lax.dot_general(
        jnp.concatenate([gain_one_term, gain_two_term], axis=0),
        reorder.astype(F32),
        (LAST, ((), ())),
        precision=lax.Precision.HIGHEST,
    )
    gain_term = jnp.concatenate([layer_terms.reshape(-1), head_terms[:2].reshape(-1)])

    sums = jnp.concatenate([*heads_sums, *inner_sums], axis=1)
    kept = core_pick(sums[:32], sums[32:])
    got = swap(core_pick(sums[32:], sums[:32]))
    by_core = (core_pick(kept, got), core_pick(got, kept))
    heads_at = ((0, 2 * HD), (2 * HD, HD), (3 * HD, HD), (4 * HD, 2 * HD))
    projections = []
    for m in range(7):
        pieces = []
        for c in range(2):
            for i in range(4):
                if m < 4:
                    start, width = heads_at[m]
                    start = start + i * HW
                else:
                    width = FF // 8
                    start = 4 * HW + i * IW + (m - 4) * width
                pieces.append(by_core[c][:, start : start + width])
        pieces.append(jnp.zeros((32, FF - WIDTHS[m]), LOW))
        projections.append(jnp.concatenate(pieces, axis=1))
    routed = []
    for mask in MASKS:
        for j in range(2):
            slot = jnp.bitwise_xor(group, mask) * 2 + j
            held = jnp.zeros((32, FF), LOW)
            for m in range(7):
                held = jnp.where(matrix_slot[m] == slot, projections[m], held)
            routed.append(held)
    routed = jnp.stack(routed)
    weight_grad = jnp.concatenate(scatter_group([routed[:, :16], routed[:, 16:]]), axis=1)

    own_ids = group * 2 + jnp.arange(2, dtype=jnp.int32)
    own_width = jnp.zeros((2,), jnp.int32)
    for m in range(7):
        own_width = own_width + jnp.where(own_ids == matrix_slot[m], WIDTHS[m], 0).astype(jnp.int32)
    column_mask = (jnp.arange(FF, dtype=jnp.int32)[None, :] < own_width[:, None]).astype(F32)
    column_mask = column_mask[:, None, :]
    momentum_new = column_mask * (momentum_keep * momentum_slots + weight_grad)
    direction = (weight_grad + momentum_keep * momentum_new).astype(LOW)

    mine = core_pick(direction[0], direction[1])
    got = swap(core_pick(direction[1], direction[0]))
    rows = core_pick(jnp.concatenate([mine, got], axis=0), jnp.concatenate([got, mine], axis=0))
    QW = FF // 4
    matrix = gather_quarters([rows[:, i * QW : (i + 1) * QW] for i in range(4)])
    *matrix, gain_term = together([*matrix, gain_term])
    gram = sum(dot(x, x, LAST) for x in matrix)
    eye = (column == source).astype(F32)
    inverse = 1.0 / (jnp.sqrt(jnp.sum(gram * eye)) + frob_eps)
    gram = gram * (inverse * inverse)
    own_rows = eye[:64]
    for sweep in range(NS_ITERS):
        gram_high, gram_low = split_two(gram)
        if sweep == NS_ITERS - 1:
            once = in_two(own_rows, gram_high)
            twice = in_two(once, gram_high)
            own_rows = coef_linear * own_rows + coef_square * once + coef_quartic * twice
            break
        square = dot(gram_high, gram_high)
        poly = (coef_square * gram_high.astype(F32) + coef_quartic * square).astype(LOW)
        if sweep == 0:
            own_rows = coef_linear * own_rows + poly[:64].astype(F32)
        else:
            own_rows = coef_linear * own_rows + in_two(own_rows, poly)
        mixed = dot(gram_high, poly) + dot(gram_low, poly)
        mixed_high, mixed_low = split_two(mixed)
        gram = (
            (coef_linear * coef_linear) * gram
            + (2.0 * coef_linear) * mixed
            + (dot(mixed_high, poly) + dot(mixed_low, poly))
        )
    own_rows = own_rows * inverse
    iterate = jnp.concatenate([in_two(own_rows, x) for x in matrix], axis=1).astype(LOW)
    kept = core_pick(iterate[:32], iterate[32:])
    got = swap(core_pick(iterate[32:], iterate[:32]))
    iterate = jnp.stack([core_pick(kept, got), core_pick(got, kept)]).astype(F32)
    update_scale = 0.2 * jnp.sqrt(jnp.maximum(own_width, D).astype(F32))
    weight_new = column_mask * (
        weight_slots * (1.0 - learn_rate * weight_decay)
        - learn_rate * update_scale[:, None, None] * iterate
    )

    gain_grad = sum_everywhere(gain_term)
    gain_momentum_new = momentum_keep * gain_momentum + gain_grad
    gain_step = gain_grad + momentum_keep * gain_momentum_new
    bounds = (0, D, 2 * D, 2 * D + HD, 2 * D + 2 * HD)
    scaled_parts = []
    for number in range(4):
        segment = gain_step[bounds[number] : bounds[number + 1]]
        scaled_parts.append(segment * lax.rsqrt(jnp.mean(segment * segment) + norm_eps))
    gain_new = gains - gain_rate * jnp.concatenate(scaled_parts)
    shape = (slot_count, length, D)
    return (
        hidden_out.reshape(shape),
        in_grad.reshape(shape),
        weight_grad,
        momentum_new,
        weight_new,
        gain_grad,
        gain_momentum_new,
        gain_new,
    )


def solution(mesh):
    finer = Mesh(
        mesh.devices.reshape(4, 4, 2, mesh.shape["group"]), ("dp_0", "dp_1", "dp_2", "group")
    )
    in_specs = (
        P(DP_GROUP, None, None),
        P(DP_GROUP, None, None),
        P(),
        P(DP_GROUP, None),
        P(),
        P("group", ("dp_0", "dp_1", "dp_2"), None),
        P("group", ("dp_0", "dp_1", "dp_2"), None),
        P(),
        P(),
    )
    out_specs = (
        P(DP_GROUP, None, None),
        P(DP_GROUP, None, None),
        P("group", ("dp_0", "dp_1", "dp_2"), None),
        P("group", ("dp_0", "dp_1", "dp_2"), None),
        P("group", ("dp_0", "dp_1", "dp_2"), None),
        P(),
        P(),
        P(),
    )
    return jax.shard_map(
        shards, mesh=finer, in_specs=in_specs, out_specs=out_specs, check_vma=False
    )
```

```python
import jax
import jax.numpy as jnp
import numpy as np
from jax import lax
from jax.experimental import pallas as pl
from jax.experimental.pallas import tpu as pltpu
from jax.sharding import Mesh
from jax.sharding import PartitionSpec as P

D = 1024
HEADS = 16
KV = 8
HD = 128
FF = 3072
SEQ = 128
NS_ITERS = 5
WIDTHS = (HEADS * HD, KV * HD, KV * HD, HEADS * HD, FF, FF, FF)
DP_GROUP = ("dp_0", "dp_1", "dp_2", "group")
LOW = jnp.bfloat16
F32 = jnp.float32

norm_eps = 1e-06
frob_eps = 1e-07
rope_base = 1000000.0
coef_linear = 3.4445
coef_square = -4.775
coef_quartic = 2.0315
momentum_keep = 0.95
learn_rate = 0.15
weight_decay = 0.1
gain_rate = 0.5
masked_score = -1e30
score_scale = HD ** (-0.5)

NEAR = ((0, 1), (1, 0), (2, 3), (3, 2))
FAR = ((0, 3), (3, 0), (1, 2), (2, 1))
LINKS = (("dp_0", NEAR), ("dp_1", NEAR), ("dp_0", FAR), ("dp_1", FAR))
MASKS = (0, 3, 1, 2)


def place_of(mask):
    return jnp.where(mask == 0, 0, jnp.where(mask == 3, 1, mask + 1))


def swap(x):
    return lax.ppermute(x, "dp_2", ((0, 1), (1, 0)))


def together(arrays):
    return list(lax.optimization_barrier(tuple(arrays)))


def gather_step(quarters, step):
    fresh = []
    for i in range(4):
        axis, pairs = LINKS[(step + i) % 4]
        fresh.append(lax.ppermute(quarters[i], axis, pairs))
    fresh = together(fresh)
    return [
        jnp.concatenate([quarters[i], fresh[i]], axis=(step + i) % 4) for i in range(4)
    ]


def gather_shaped(x, width):
    return [
        x[:, i * width : (i + 1) * width].reshape(1, 1, 1, 1, x.shape[0], width) for i in range(4)
    ]


def flat(quarters):
    return [q.reshape(-1, q.shape[-1]) for q in quarters]


def scatter_step(sent, kept, step):
    to_send, to_keep, came = [], [], []
    for i in range(4):
        axis, pairs = LINKS[(step + i) % 4]
        came.append(lax.ppermute(sent[i], axis, pairs))
    came = together(came)
    for i in range(4):
        got = came[i]
        half = got.shape[0] // 2 if step < 3 else got.shape[0]
        to_keep.append((kept[i][:half].astype(F32) + got[:half].astype(F32)).astype(LOW))
        to_send.append((kept[i][half:].astype(F32) + got[half:].astype(F32)).astype(LOW))
    return to_send, to_keep


def gather_group(halves):
    held = [h[None, None] for h in halves]
    for step in range(2):
        fresh = [lax.ppermute(held[i], "group", (NEAR, FAR)[(step + i) % 2]) for i in range(2)]
        held = [jnp.concatenate([held[i], fresh[i]], axis=(step + i) % 2) for i in range(2)]
    return [h.reshape(8, *h.shape[3:]) for h in held]


def dot(left, right, dims=((1,), (0,))):
    return lax.dot_general(left, right, (dims, ((), ())), preferred_element_type=F32)


ROWS = ((0,), (0,))
LAST = ((1,), (1,))
PLAIN = ((1,), (0,))


def split_two(x):
    high = lax.reduce_precision(x, exponent_bits=8, mantissa_bits=7)
    return high.astype(LOW), (x - high).astype(LOW)


def half_turn(u):
    return jnp.concatenate([u[:, HD // 2 :], u[:, : HD // 2]], axis=1)


def head_forward(raw, gain, cosine, sine):
    scale = lax.rsqrt(jnp.mean(raw * raw, axis=-1, keepdims=True) + norm_eps)
    normed = raw * scale
    gained = normed * gain
    turned = gained * cosine + half_turn(gained) * sine
    return normed, scale, turned.astype(LOW)


def softmax_parts(query, key):
    scores = dot(query, key, LAST) * score_scale
    rows = lax.broadcasted_iota(jnp.int32, scores.shape, 0) & (SEQ - 1)
    columns = lax.broadcasted_iota(jnp.int32, scores.shape, 1)
    scores = jnp.where(rows >= columns, scores, masked_score)
    terms = jnp.exp(scores - jnp.max(scores, axis=-1, keepdims=True))
    return terms / jnp.sum(terms, axis=-1, keepdims=True)


def two_heads(ref, at):
    return jnp.concatenate([ref[at, :HD], ref[at, HD : 2 * HD]], axis=0)


def twice(x):
    return jnp.concatenate([x, x], axis=0)


def heads_kernel(
    input_ref, weight_ref, cos_ref, sin_ref, gain_ref, sum_ref, raw_ref, attn_ref, out_ref
):
    raw_ref[...] = dot(input_ref[...], weight_ref[:, : 4 * HD])
    for b in range(raw_ref.shape[0] // SEQ):
        at = slice(b * SEQ, (b + 1) * SEQ)
        cosine, sine = cos_ref[at, :], sin_ref[at, :]
        _, _, key = head_forward(raw_ref[at, 2 * HD : 3 * HD], gain_ref[1:2, :], cosine, sine)
        value = raw_ref[at, 3 * HD :].astype(LOW)
        _, _, query = head_forward(
            two_heads(raw_ref, at), gain_ref[0:1, :], twice(cosine), twice(sine)
        )
        probs = softmax_parts(query, key).astype(LOW)
        out = dot(probs, value).astype(LOW)
        attn_ref[at, :HD] = out[:SEQ]
        attn_ref[at, HD:] = out[SEQ:]
    out_ref[...] = sum_ref[...] + dot(attn_ref[...], weight_ref[:, 4 * HD :], LAST)


def head_backward(grad, normed, scale, gain, cosine, sine):
    back = grad * cosine - half_turn(grad) * sine
    term = jnp.sum(back * normed, axis=0, keepdims=True)
    g = back * gain
    raw = scale * (g - normed * jnp.mean(g * normed, axis=-1, keepdims=True))
    return raw.astype(LOW), term


def heads_back_kernel(
    raw_ref,
    branch_ref,
    weight_ref,
    cos_ref,
    sin_ref,
    gain_ref,
    sum_ref,
    out_ref,
    term_ref,
    one_ref,
    grad_ref,
):
    grad_ref[...] = dot(branch_ref[...], weight_ref[:, 4 * HD :]).astype(LOW)
    query_terms, key_terms = 0.0, 0.0
    for b in range(raw_ref.shape[0] // SEQ):
        at = slice(b * SEQ, (b + 1) * SEQ)
        cosine, sine = cos_ref[at, :], sin_ref[at, :]
        cosines, sines = twice(cosine), twice(sine)
        key_hat, key_scale, key = head_forward(
            raw_ref[at, 2 * HD : 3 * HD], gain_ref[1:2, :], cosine, sine
        )
        value = raw_ref[at, 3 * HD :].astype(LOW)
        query_hat, query_scale, query = head_forward(
            two_heads(raw_ref, at), gain_ref[0:1, :], cosines, sines
        )
        probs = softmax_parts(query, key)
        grad_attn = two_heads(grad_ref, at)
        grad_value = dot(probs.astype(LOW), grad_attn, ROWS)
        grad_probs = dot(grad_attn, value, LAST)
        inner = jnp.sum(probs * grad_probs, axis=-1, keepdims=True)
        grad_scores = (probs * (grad_probs - inner)).astype(LOW)
        grad_query = dot(grad_scores, key) * score_scale
        grad_key = dot(grad_scores, query, ROWS) * score_scale
        raw, term = head_backward(
            grad_query, query_hat, query_scale, gain_ref[0:1, :], cosines, sines
        )
        query_terms = query_terms + term
        out_ref[at, :HD] = raw[:SEQ]
        out_ref[at, HD : 2 * HD] = raw[SEQ:]
        raw, term = head_backward(grad_key, key_hat, key_scale, gain_ref[1:2, :], cosine, sine)
        key_terms = key_terms + term
        out_ref[at, 2 * HD : 3 * HD] = raw
        out_ref[at, 3 * HD :] = grad_value.astype(LOW)
    spare = jnp.zeros((6, HD), F32)
    term_ref[...] = jnp.concatenate([query_terms, key_terms, spare], axis=0)
    one_ref[...] = sum_ref[...] + dot(out_ref[...], weight_ref[:, : 4 * HD], LAST)


BLOCK = D // 4


def iterate_kernel(x0, x1, x2, x3, out_ref, gram, high, low, poly, mixed_high, mixed_low, own):
    at = [slice(i * BLOCK, (i + 1) * BLOCK) for i in range(4)]
    blocks = [(i, j) for i in range(4) for j in range(4)]

    def parts(x):
        top = x.astype(LOW)
        return top, (x - top.astype(F32)).astype(LOW)

    def mirrored(ref, i, j, block):
        ref[at[i], at[j]] = block.astype(ref.dtype)
        if i != j:
            ref[at[j], at[i]] = block.T.astype(ref.dtype)

    def two_dot(left, right):
        rows = left.shape[0]
        both_parts = dot(jnp.concatenate(parts(left), axis=0), right)
        return both_parts[:rows] + both_parts[rows:]

    rows = lax.broadcasted_iota(jnp.int32, (BLOCK, BLOCK), 0)
    columns = lax.broadcasted_iota(jnp.int32, (BLOCK, BLOCK), 1)
    trace = jnp.zeros((1, 1), F32)
    for i, j in blocks:
        if j > i:
            continue
        block = sum(dot(x[at[i], :], x[at[j], :], LAST) for x in (x0, x1, x2, x3))
        mirrored(gram, i, j, block)
        if i == j:
            diagonal = jnp.where(rows == columns, block, 0.0)
            trace = trace + jnp.sum(jnp.sum(diagonal, axis=1, keepdims=True), axis=0, keepdims=True)
    inverse = 1.0 / (jnp.sqrt(trace) + frob_eps)
    for i, j in blocks:
        block = gram[at[i], at[j]] * (inverse * inverse)
        gram[at[i], at[j]] = block
        high[at[i], at[j]], low[at[i], at[j]] = parts(block)
    own_rows = lax.broadcasted_iota(jnp.int32, own.shape, 0)
    own[...] = (own_rows == lax.broadcasted_iota(jnp.int32, own.shape, 1)).astype(F32)

    def sweep(_, carry):
        for i, j in blocks:
            if j > i:
                continue
            square = dot(high[at[i], :], high[:, at[j]])
            block = coef_square * high[at[i], at[j]].astype(F32) + coef_quartic * square
            mirrored(poly, i, j, block)
        own[...] = coef_linear * own[...] + two_dot(own[...], poly[...])
        for i, j in blocks:
            block = dot(high[at[i], :], poly[:, at[j]]) + dot(low[at[i], :], poly[:, at[j]])
            gram[at[i], at[j]] = (coef_linear * coef_linear) * gram[at[i], at[j]] + (
                2.0 * coef_linear
            ) * block
            mixed_high[at[i], at[j]], mixed_low[at[i], at[j]] = parts(block)
        for i, j in blocks:
            block = dot(mixed_high[at[i], :], poly[:, at[j]])
            block = block + dot(mixed_low[at[i], :], poly[:, at[j]]) + gram[at[i], at[j]]
            gram[at[i], at[j]] = block
            high[at[i], at[j]], low[at[i], at[j]] = parts(block)
        return carry

    lax.fori_loop(0, NS_ITERS - 1, sweep, 0)
    once = two_dot(own[...], high[...])
    second = two_dot(once, high[...])
    last = coef_linear * own[...] + coef_square * once + coef_quartic * second
    last = last * inverse
    for k, x in enumerate((x0, x1, x2, x3)):
        width = x.shape[1]
        out_ref[:, k * width : (k + 1) * width] = two_dot(last, x[...]).astype(LOW)


def iterate_rows(matrix):
    in_vmem = pl.BlockSpec(memory_space=pltpu.VMEM)
    square = pltpu.VMEM((D, D), LOW)
    return pl.pallas_call(
        iterate_kernel,
        in_specs=[in_vmem] * 4,
        out_specs=in_vmem,
        out_shape=jax.ShapeDtypeStruct((64, FF), LOW),
        scratch_shapes=[pltpu.VMEM((D, D), F32), *[square] * 5, pltpu.VMEM((64, D), F32)],
        compiler_params=pltpu.CompilerParams(vmem_limit_bytes=48 * 2**20),
        cost_estimate=pl.CostEstimate(flops=50 * 10**9, bytes_accessed=2**23, transcendentals=0),
    )(*matrix)


def by_sequence(width):
    return pl.BlockSpec((2 * SEQ, width), lambda s: (s, 0))


def whole(rows, width):
    return pl.BlockSpec((rows, width), lambda s: (0, 0))


SMALL = pl.CostEstimate(flops=2**20, bytes_accessed=2**16, transcendentals=0)
KERNEL_SPACE = pltpu.CompilerParams(vmem_limit_bytes=32 * 2**20)


def heads_forward(inputs, weight, cosine, sine, gain_rows, total):
    tokens = inputs.shape[0]
    return pl.pallas_call(
        heads_kernel,
        grid=(tokens // (2 * SEQ),),
        in_specs=[
            by_sequence(D),
            whole(D, 6 * HD),
            by_sequence(HD),
            by_sequence(HD),
            whole(8, HD),
            by_sequence(D),
        ],
        out_specs=[by_sequence(4 * HD), by_sequence(2 * HD), by_sequence(D)],
        out_shape=[
            jax.ShapeDtypeStruct((tokens, 4 * HD), F32),
            jax.ShapeDtypeStruct((tokens, 2 * HD), LOW),
            jax.ShapeDtypeStruct((tokens, D), F32),
        ],
        compiler_params=KERNEL_SPACE,
        cost_estimate=SMALL,
    )(inputs, weight, cosine, sine, gain_rows, total)


def heads_backward(raw, branch, weight, cosine, sine, gain_rows, total):
    tokens = raw.shape[0]
    grad_raw, terms, total = pl.pallas_call(
        heads_back_kernel,
        grid=(tokens // (2 * SEQ),),
        in_specs=[
            by_sequence(4 * HD),
            by_sequence(D),
            whole(D, 6 * HD),
            by_sequence(HD),
            by_sequence(HD),
            whole(8, HD),
            by_sequence(D),
        ],
        out_specs=[
            by_sequence(4 * HD),
            pl.BlockSpec((8, HD), lambda s: (s, 0)),
            by_sequence(D),
        ],
        out_shape=[
            jax.ShapeDtypeStruct((tokens, 4 * HD), LOW),
            jax.ShapeDtypeStruct((tokens // (2 * SEQ) * 8, HD), F32),
            jax.ShapeDtypeStruct((tokens, D), F32),
        ],
        scratch_shapes=[pltpu.VMEM((2 * SEQ, 2 * HD), LOW)],
        compiler_params=KERNEL_SPACE,
        cost_estimate=SMALL,
    )(raw, branch, weight, cosine, sine, gain_rows, total)
    return grad_raw, jnp.sum(terms.reshape(-1, 8, HD), axis=0), total


def shared_sum(partial):
    own = partial.shape[0] // 2
    return partial[:own] + swap(partial[own:].astype(LOW)).astype(F32)


def both(x):
    return jnp.concatenate([x, swap(x)], axis=0)


def norm_back(grad_hat, normed, scale):
    return scale * (grad_hat - normed * jnp.mean(grad_hat * normed, axis=-1, keepdims=True))


HEADS_WIDTH, INNER_WIDTH = 6 * HD, 3 * FF // 8


def pieces_of(core):
    pieces = []
    for i in range(core * 4, core * 4 + 4):
        pieces += [(0, i * 2 * HD, 2 * HD), (1, i * HD, HD), (2, i * HD, HD), (3, i * 2 * HD, 2 * HD)]
    for i in range(core * 4, core * 4 + 4):
        pieces += [(m, i * FF // 8, FF // 8) for m in (4, 5, 6)]
    return pieces


HALF_WIDTH = sum(WIDTHS) // 2


def compact_kernel(at_ref, top_ref, low_ref, mine_ref, theirs_ref):
    for core in range(2):

        @pl.when(at_ref[7] == core)
        def _():
            for out_ref, pieces in ((mine_ref, pieces_of(core)), (theirs_ref, pieces_of(1 - core))):
                to = 0
                for m, start, width in pieces:
                    out_ref[:16, to : to + width] = top_ref[at_ref[m], :, start : start + width]
                    out_ref[16:, to : to + width] = low_ref[at_ref[m], :, start : start + width]
                    to += width


def compact(at, top, low):
    half = jax.ShapeDtypeStruct((32, HALF_WIDTH), LOW)
    in_vmem = pl.BlockSpec(memory_space=pltpu.VMEM)
    return pl.pallas_call(
        compact_kernel,
        in_specs=[pl.BlockSpec(memory_space=pltpu.SMEM), in_vmem, in_vmem],
        out_specs=[in_vmem, in_vmem],
        out_shape=[half, half],
        compiler_params=pltpu.CompilerParams(vmem_limit_bytes=24 * 2**20),
        cost_estimate=pl.CostEstimate(flops=0, bytes_accessed=5 * 2**20, transcendentals=0),
    )(at, top, low)


def route_kernel(of_ref, kept_ref, got_ref, top_keep, top_send, low_keep, low_send, held):
    held[...] = jnp.zeros_like(held)
    for core in range(2):

        @pl.when(of_ref[8] == core)
        def _():
            for in_ref, pieces in ((kept_ref, pieces_of(core)), (got_ref, pieces_of(1 - core))):
                at = 0
                for m, start, width in pieces:
                    held[m, :, start : start + width] = in_ref[:, at : at + width]
                    at += width

    for place in range(8):
        near, far, j = place // 4, (place // 2) % 2, place % 2
        (top_keep, top_send)[near][2 * far + j] = held[of_ref[place], :16, :]
        (low_keep, low_send)[far][2 * near + j] = held[of_ref[place], 16:, :]


def route(of, kept, got):
    half = jax.ShapeDtypeStruct((4, 16, FF), LOW)
    in_vmem = pl.BlockSpec(memory_space=pltpu.VMEM)
    return pl.pallas_call(
        route_kernel,
        in_specs=[pl.BlockSpec(memory_space=pltpu.SMEM), in_vmem, in_vmem],
        out_specs=[in_vmem] * 4,
        out_shape=[half] * 4,
        scratch_shapes=[pltpu.VMEM((8, 32, FF), LOW)],
        compiler_params=pltpu.CompilerParams(vmem_limit_bytes=24 * 2**20),
        cost_estimate=pl.CostEstimate(flops=0, bytes_accessed=5 * 2**20, transcendentals=0),
    )(of, kept, got)


def turned_source():
    at = np.arange(D).reshape(2, 2, 2, 2, 64)
    turns = [np.transpose(at, [*(np.arange(4) + i) % 4, 4]).reshape(-1) for i in (1, 2, 3)]
    return np.concatenate(turns).astype(np.int32)


def shards(
    hidden_in,
    out_grad,
    seq_owner,
    token_place,
    matrix_slot,
    weight_slots,
    momentum_slots,
    gains,
    gain_momentum,
):
    slot_count, length = hidden_in.shape[:2]
    tok_count = slot_count * length
    z, y = lax.axis_index("dp_0"), lax.axis_index("dp_1")
    core, group = lax.axis_index("dp_2"), lax.axis_index("group")
    first_core = core == 0
    replica = ((z * 4 + y) * 2 + core) * 4 + group

    def core_pick(zero, one):
        return jnp.where(first_core, zero, one)

    weight_low = weight_slots.astype(LOW)
    slots_top, slots_low = gather_group([weight_low[:, :16], weight_low[:, 16:]])
    at = place_of(jnp.bitwise_xor(group, matrix_slot >> 1)) * 2 + (matrix_slot & 1)
    mine, theirs = compact(jnp.concatenate([at, core[None]]), slots_top, slots_low)
    got = swap(theirs)
    chip_rows = core_pick(
        jnp.concatenate([mine, got], axis=0), jnp.concatenate([got, mine], axis=0)
    )
    heads_held = gather_shaped(chip_rows[:, : 4 * HEADS_WIDTH], HEADS_WIDTH)
    inner_held = gather_shaped(chip_rows[:, 4 * HEADS_WIDTH :], INNER_WIDTH)
    heads_held = together(gather_step(heads_held, 0))
    held = together([*gather_step(heads_held, 1), *inner_held])
    held = together([*gather_step(held[:4], 2), *gather_step(held[4:], 0)])
    held = together([*gather_step(held[:4], 3), *gather_step(held[4:], 1)])
    w_heads, inner_held = flat(held[:4]), held[4:]
    inner_held = gather_step(inner_held, 2)
    held = together([*inner_held, *w_heads[1:]])
    inner_held, w_heads = held[:4], [w_heads[0], *held[4:]]
    w_inner = flat(gather_step(inner_held, 3))
    w_gate_up = [w[:, : FF // 4] for w in w_inner]
    w_down = [w[:, FF // 4 :] for w in w_inner]

    column = lax.broadcasted_iota(jnp.int32, (D, D), 1)
    source = lax.broadcasted_iota(jnp.int32, (D, D), 0)
    block = column // 64
    near_z, near_y = block // 8, (block // 4) % 2
    far_z, far_y = (block // 2) % 2, block % 2
    from_z = jnp.bitwise_xor(z, jnp.bitwise_xor(near_z, far_z * 3))
    from_y = jnp.bitwise_xor(y, jnp.bitwise_xor(near_y, far_y * 3))
    reorder = (source == (from_z * 4 + from_y) * 64 + column % 64).astype(LOW)

    turn_source = jnp.asarray(turned_source())[None, :]
    turn = (lax.broadcasted_iota(jnp.int32, (D, 3 * D), 0) == turn_source).astype(LOW)

    def led_by_each(x):
        rest = dot(x, turn).astype(LOW)
        return [x, *(rest[:, i * D : (i + 1) * D] for i in range(3))]

    live_count = jnp.sum((seq_owner == replica).astype(jnp.int32))
    live_slot = (jnp.arange(slot_count, dtype=jnp.int32) < live_count).astype(F32)
    live_token = jnp.repeat(live_slot, length)[:, None]
    tokens = dot(hidden_in.reshape(tok_count, D), reorder)
    grad_out = dot(out_grad.reshape(tok_count, D), reorder) * live_token
    grad_low = both(grad_out.astype(LOW))
    grad_led = led_by_each(grad_low)
    layer_gains = jnp.dot(
        gains[: 2 * D].reshape(2, D), reorder.astype(F32), precision=lax.Precision.HIGHEST
    )
    gain_one, gain_two = layer_gains[0:1], layer_gains[1:2]
    gain_rows = jnp.pad(gains[2 * D :].reshape(2, HD), ((0, 6), (0, 0)))
    places = both(token_place).astype(F32).reshape(-1, 1)
    exponent = jnp.arange(HD // 2, dtype=F32) * (-2.0 / HD)
    angles = places * jnp.power(rope_base, exponent)[None, :]
    cosine, sine = jnp.cos(angles), jnp.sin(angles)
    cosine = jnp.concatenate([cosine, cosine], axis=1)
    sine = jnp.concatenate([-sine, sine], axis=1)

    scale_one = lax.rsqrt(jnp.mean(tokens * tokens, axis=-1, keepdims=True) + norm_eps)
    normed_one = tokens * scale_one
    input_one = both((normed_one * gain_one).astype(LOW))
    one_led = led_by_each(input_one)
    raw, attn = [], []
    branch = jnp.zeros((2 * tok_count, D), F32)
    for w in w_heads:
        fresh, heads, branch = heads_forward(input_one, w, cosine, sine, gain_rows, branch)
        raw.append(fresh)
        attn.append(heads)
    residual = tokens + shared_sum(branch)
    scale_two = lax.rsqrt(jnp.mean(residual * residual, axis=-1, keepdims=True) + norm_eps)
    normed_two = residual * scale_two
    input_two = both((normed_two * gain_two).astype(LOW))
    two_led = led_by_each(input_two)
    act, grad_inner, grad_two = [], [], 0.0
    outward = 0.0
    for i in range(4):
        gate_up = dot(input_two, w_gate_up[i])
        gate, up = gate_up[:, : FF // 8], gate_up[:, FF // 8 :]
        sigmoid = jax.nn.sigmoid(gate)
        swish = gate * sigmoid
        act.append((swish * up).astype(LOW))
        grad_act = dot(grad_low, w_down[i])
        slope = sigmoid * (1.0 + gate * (1.0 - sigmoid))
        grad_inner.append(
            jnp.concatenate(
                [(grad_act * up * slope).astype(LOW), (grad_act * swish).astype(LOW)], axis=1
            )
        )
        outward = outward + dot(act[i], w_down[i], LAST)
        grad_two = grad_two + dot(grad_inner[i], w_gate_up[i], LAST)
    result = (residual + shared_sum(outward)) * live_token
    hidden_out = dot(result.astype(LOW), reorder, LAST).astype(LOW)

    def halves_of(first_left, first_right, second_left, second_right):
        sent, kept = [], []
        for i in range(4):
            for half, out in ((slice(D // 2, D), sent), (slice(0, D // 2), kept)):
                first = dot(first_left[i][:, half], first_right[i], ROWS)
                second = dot(second_left[i][:, half], second_right[i], ROWS)
                out.append(jnp.concatenate([first.astype(LOW), second.astype(LOW)], axis=1))
        return sent, kept

    sent, kept = halves_of(two_led, grad_inner, grad_led, act)
    grad_two = shared_sum(grad_two)
    gain_two_term = jnp.sum(grad_two * normed_two, axis=0, keepdims=True)
    grad_residual = grad_out + norm_back(grad_two * gain_two, normed_two, scale_two)
    branch_low = both(grad_residual.astype(LOW))
    branch_led = led_by_each(branch_low)
    grad_one, head_terms, grad_raw = jnp.zeros((2 * tok_count, D), F32), 0.0, []
    branch_now = branch_low
    for i in range(4):
        fresh, term, grad_one = heads_backward(
            raw[i], branch_now, w_heads[i], cosine, sine, gain_rows, grad_one
        )
        grad_raw.append(fresh)
        head_terms = head_terms + term
        sent, kept = scatter_step(sent, kept, i)
        if i < 3:
            *held, branch_now = together([*sent, *kept, branch_now])
            sent, kept = held[:4], held[4:]
    inner_sums = kept
    sent, kept = halves_of(one_led, grad_raw, branch_led, attn)
    for step in range(4):
        sent, kept = scatter_step(sent, kept, step)
        if step < 3:
            held = together([*sent, *kept])
            sent, kept = held[:4], held[4:]
    heads_sums = kept
    grad_one = shared_sum(grad_one)
    gain_one_term = jnp.sum(grad_one * normed_one, axis=0, keepdims=True)
    in_grad = grad_residual + norm_back(grad_one * gain_one, normed_one, scale_one)
    in_high, in_low = split_two(in_grad)
    in_grad = dot(in_high, reorder, LAST) + dot(in_low, reorder, LAST)
    layer_terms = lax.dot_general(
        jnp.concatenate([gain_one_term, gain_two_term], axis=0),
        reorder.astype(F32),
        (LAST, ((), ())),
        precision=lax.Precision.HIGHEST,
    )
    gain_sum = jnp.concatenate([layer_terms.reshape(-1), head_terms[:2].reshape(-1)])

    sums = jnp.concatenate([*heads_sums, *inner_sums], axis=1)
    kept = core_pick(sums[:32], sums[32:])
    got = swap(core_pick(sums[32:], sums[:32]))
    slot_at = (jnp.bitwise_xor(group, jnp.asarray(MASKS, jnp.int32)) * 2)[:, None]
    slot_at = (slot_at + jnp.arange(2, dtype=jnp.int32)[None, :]).reshape(8)
    matches = slot_at[:, None] == matrix_slot[None, :]
    numbers = jnp.arange(7, dtype=jnp.int32)[None, :]
    routed_from = 7 - jnp.max(jnp.where(matches, 7 - numbers, 0), axis=1)
    halves = route(jnp.concatenate([routed_from, core[None]]), kept, got)
    sent, kept = [halves[1], halves[3]], [halves[0], halves[2]]
    for step in range(2):
        got = [lax.ppermute(sent[i], "group", (NEAR, FAR)[(step + i) % 2]) for i in range(2)]
        gain_sum = gain_sum + lax.ppermute(gain_sum, "group", (NEAR, FAR)[step])
        total = [kept[i].astype(F32) + got[i].astype(F32) for i in range(2)]
        if step == 0:
            *held, gain_sum = together(
                [*(t[2:].astype(LOW) for t in total), *(t[:2].astype(LOW) for t in total), gain_sum]
            )
            sent, kept = held[:2], held[2:]
    weight_grad = jnp.concatenate(total, axis=1)

    own_ids = group * 2 + jnp.arange(2, dtype=jnp.int32)
    own_match = own_ids[:, None] == matrix_slot[None, :]
    own_width = jnp.sum(jnp.where(own_match, jnp.asarray(WIDTHS, jnp.int32)[None, :], 0), axis=1)
    own_width = own_width.astype(jnp.int32)
    column_mask = (jnp.arange(FF, dtype=jnp.int32)[None, :] < own_width[:, None]).astype(F32)
    column_mask = column_mask[:, None, :]
    momentum_new = column_mask * (momentum_keep * momentum_slots + weight_grad)
    direction = (weight_grad + momentum_keep * momentum_new).astype(LOW)

    mine = core_pick(direction[0], direction[1])
    got = swap(core_pick(direction[1], direction[0]))
    rows = core_pick(jnp.concatenate([mine, got], axis=0), jnp.concatenate([got, mine], axis=0))
    held = gather_shaped(rows, FF // 4)
    gain_sum = gain_sum + swap(gain_sum)
    for step in range(4):
        gain_sum = gain_sum + lax.ppermute(gain_sum, *LINKS[step])
        *held, gain_sum = together([*gather_step(held, step), gain_sum])
    matrix, gain_grad = flat(held), gain_sum
    iterate = iterate_rows(matrix)
    kept = core_pick(iterate[:32], iterate[32:])
    got = swap(core_pick(iterate[32:], iterate[:32]))
    iterate = jnp.stack([core_pick(kept, got), core_pick(got, kept)]).astype(F32)
    update_scale = 0.2 * jnp.sqrt(jnp.maximum(own_width, D).astype(F32))
    weight_new = column_mask * (
        weight_slots * (1.0 - learn_rate * weight_decay)
        - learn_rate * update_scale[:, None, None] * iterate
    )

    gain_momentum_new = momentum_keep * gain_momentum + gain_grad
    gain_step = gain_grad + momentum_keep * gain_momentum_new
    bounds = (0, D, 2 * D, 2 * D + HD, 2 * D + 2 * HD)
    scaled_parts = []
    for number in range(4):
        segment = gain_step[bounds[number] : bounds[number + 1]]
        scaled_parts.append(segment * lax.rsqrt(jnp.mean(segment * segment) + norm_eps))
    gain_new = gains - gain_rate * jnp.concatenate(scaled_parts)
    shape = (slot_count, length, D)
    return (
        hidden_out.reshape(shape),
        in_grad.reshape(shape),
        weight_grad,
        momentum_new,
        weight_new,
        gain_grad,
        gain_momentum_new,
        gain_new,
    )


def solution(mesh):
    finer = Mesh(
        mesh.devices.reshape(4, 4, 2, mesh.shape["group"]), ("dp_0", "dp_1", "dp_2", "group")
    )
    in_specs = (
        P(DP_GROUP, None, None),
        P(DP_GROUP, None, None),
        P(),
        P(DP_GROUP, None),
        P(),
        P("group", ("dp_0", "dp_1", "dp_2"), None),
        P("group", ("dp_0", "dp_1", "dp_2"), None),
        P(),
        P(),
    )
    out_specs = (
        P(DP_GROUP, None, None),
        P(DP_GROUP, None, None),
        P("group", ("dp_0", "dp_1", "dp_2"), None),
        P("group", ("dp_0", "dp_1", "dp_2"), None),
        P("group", ("dp_0", "dp_1", "dp_2"), None),
        P(),
        P(),
        P(),
    )
    return jax.shard_map(
        shards, mesh=finer, in_specs=in_specs, out_specs=out_specs, check_vma=False
    )
```

```python
import functools

import jax
import jax.numpy as jnp
from jax import lax
from jax.experimental import pallas as pl
from jax.experimental.pallas import tpu as pltpu
from jax.sharding import Mesh
from jax.sharding import PartitionSpec as P

D = 1024
HEADS = 16
KV = 8
HD = 128
FF = 3072
SEQ = 128
NS_ITERS = 5
WIDTHS = (HEADS * HD, KV * HD, KV * HD, HEADS * HD, FF, FF, FF)
DP_GROUP = ("dp_0", "dp_1", "dp_2", "group")
LOW = jnp.bfloat16
F32 = jnp.float32

norm_eps = 1e-06
frob_eps = 1e-07
rope_base = 1000000.0
coef_linear = 3.4445
coef_square = -4.775
coef_quartic = 2.0315
momentum_keep = 0.95
learn_rate = 0.15
weight_decay = 0.1
gain_rate = 0.5
masked_score = -1e30
score_scale = HD ** (-0.5)

NEAR = ((0, 1), (1, 0), (2, 3), (3, 2))
FAR = ((0, 3), (3, 0), (1, 2), (2, 1))
LINKS = (("dp_0", NEAR), ("dp_1", NEAR), ("dp_0", FAR), ("dp_1", FAR))
MASKS = (0, 3, 1, 2)


def place_of(mask):
    return jnp.where(mask == 0, 0, jnp.where(mask == 3, 1, mask + 1))


def swap(x):
    return lax.ppermute(x, "dp_2", ((0, 1), (1, 0)))


def together(arrays):
    return list(lax.optimization_barrier(tuple(arrays)))


def gather_came(quarters, step):
    fresh = []
    for i in range(4):
        axis, pairs = LINKS[(step + i) % 4]
        fresh.append(lax.ppermute(quarters[i], axis, pairs))
    return together(fresh)


def gather_step(quarters, step):
    fresh = gather_came(quarters, step)
    return [
        jnp.concatenate([quarters[i], fresh[i]], axis=(step + i) % 4) for i in range(4)
    ]


def gather_shaped(x, width):
    return [
        x[:, i * width : (i + 1) * width].reshape(1, 1, 1, 1, x.shape[0], width) for i in range(4)
    ]


def flat(quarters):
    return [q.reshape(-1, q.shape[-1]) for q in quarters]


def scatter_step(sent, kept, step):
    to_send, to_keep, came = [], [], []
    for i in range(4):
        axis, pairs = LINKS[(step + i) % 4]
        came.append(lax.ppermute(sent[i], axis, pairs))
    came = together(came)
    for i in range(4):
        at = (step + 1 + i) % 4

        def half(part):
            if step == 3:
                return (kept[i].astype(F32) + came[i].astype(F32)).astype(LOW)
            both_parts = [lax.slice_in_dim(x, part, part + 1, axis=at) for x in (kept[i], came[i])]
            return (both_parts[0].astype(F32) + both_parts[1].astype(F32)).astype(LOW)

        to_keep.append(half(0))
        if step < 3:
            to_send.append(half(1))
    return to_send, to_keep


def gather_group(halves, after):
    held = [h[None, None] for h in halves]
    for step in range(2):
        fresh = [lax.ppermute(held[i], "group", (NEAR, FAR)[(step + i) % 2]) for i in range(2)]
        if step == 0:
            *fresh, after = together([*fresh, after])
        held = [jnp.concatenate([held[i], fresh[i]], axis=(step + i) % 2) for i in range(2)]
    return [h.reshape(8, *h.shape[3:]) for h in held], after


def dot(left, right, dims=((1,), (0,))):
    return lax.dot_general(left, right, (dims, ((), ())), preferred_element_type=F32)


ROWS = ((0,), (0,))
LAST = ((1,), (1,))
PLAIN = ((1,), (0,))


def split_two(x):
    high = lax.reduce_precision(x, exponent_bits=8, mantissa_bits=7)
    return high.astype(LOW), (x - high).astype(LOW)


def half_turn(u):
    return jnp.concatenate([u[:, HD // 2 :], u[:, : HD // 2]], axis=1)


def head_forward(raw, gain, cosine, sine):
    scale = lax.rsqrt(jnp.mean(raw * raw, axis=-1, keepdims=True) + norm_eps)
    normed = raw * scale
    gained = normed * gain
    turned = gained * cosine + half_turn(gained) * sine
    return normed, scale, turned.astype(LOW)


def softmax_parts(query, key):
    scores = dot(query, key, LAST) * score_scale
    rows = lax.broadcasted_iota(jnp.int32, scores.shape, 0) & (SEQ - 1)
    columns = lax.broadcasted_iota(jnp.int32, scores.shape, 1)
    scores = jnp.where(rows >= columns, scores, masked_score)
    terms = jnp.exp(scores - jnp.max(scores, axis=-1, keepdims=True))
    return terms / jnp.sum(terms, axis=-1, keepdims=True)


def two_heads(ref, at):
    return jnp.concatenate([ref[at, :HD], ref[at, HD : 2 * HD]], axis=0)


def twice(x):
    return jnp.concatenate([x, x], axis=0)


def heads_kernel(
    input_ref, weight_ref, cos_ref, sin_ref, gain_ref, sum_ref, raw_ref, attn_ref, out_ref
):
    raw_ref[...] = dot(input_ref[...], weight_ref[:, : 4 * HD])
    for b in range(raw_ref.shape[0] // SEQ):
        at = slice(b * SEQ, (b + 1) * SEQ)
        cosine, sine = cos_ref[at, :], sin_ref[at, :]
        _, _, key = head_forward(raw_ref[at, 2 * HD : 3 * HD], gain_ref[1:2, :], cosine, sine)
        value = raw_ref[at, 3 * HD :].astype(LOW)
        _, _, query = head_forward(
            two_heads(raw_ref, at), gain_ref[0:1, :], twice(cosine), twice(sine)
        )
        probs = softmax_parts(query, key).astype(LOW)
        out = dot(probs, value).astype(LOW)
        attn_ref[at, :HD] = out[:SEQ]
        attn_ref[at, HD:] = out[SEQ:]
    out_ref[...] = sum_ref[...] + dot(attn_ref[...], weight_ref[:, 4 * HD :], LAST)


def head_backward(grad, normed, scale, gain, cosine, sine):
    back = grad * cosine - half_turn(grad) * sine
    term = jnp.sum(back * normed, axis=0, keepdims=True)
    g = back * gain
    raw = scale * (g - normed * jnp.mean(g * normed, axis=-1, keepdims=True))
    return raw.astype(LOW), term


def heads_back_kernel(
    raw_ref,
    branch_ref,
    weight_ref,
    cos_ref,
    sin_ref,
    gain_ref,
    sum_ref,
    out_ref,
    term_ref,
    one_ref,
    grad_ref,
):
    grad_ref[...] = dot(branch_ref[...], weight_ref[:, 4 * HD :]).astype(LOW)
    query_terms, key_terms = 0.0, 0.0
    for b in range(raw_ref.shape[0] // SEQ):
        at = slice(b * SEQ, (b + 1) * SEQ)
        cosine, sine = cos_ref[at, :], sin_ref[at, :]
        cosines, sines = twice(cosine), twice(sine)
        key_hat, key_scale, key = head_forward(
            raw_ref[at, 2 * HD : 3 * HD], gain_ref[1:2, :], cosine, sine
        )
        value = raw_ref[at, 3 * HD :].astype(LOW)
        query_hat, query_scale, query = head_forward(
            two_heads(raw_ref, at), gain_ref[0:1, :], cosines, sines
        )
        probs = softmax_parts(query, key)
        grad_attn = two_heads(grad_ref, at)
        grad_value = dot(probs.astype(LOW), grad_attn, ROWS)
        grad_probs = dot(grad_attn, value, LAST)
        inner = jnp.sum(probs * grad_probs, axis=-1, keepdims=True)
        grad_scores = (probs * (grad_probs - inner)).astype(LOW)
        grad_query = dot(grad_scores, key) * score_scale
        grad_key = dot(grad_scores, query, ROWS) * score_scale
        raw, term = head_backward(
            grad_query, query_hat, query_scale, gain_ref[0:1, :], cosines, sines
        )
        query_terms = query_terms + term
        out_ref[at, :HD] = raw[:SEQ]
        out_ref[at, HD : 2 * HD] = raw[SEQ:]
        raw, term = head_backward(grad_key, key_hat, key_scale, gain_ref[1:2, :], cosine, sine)
        key_terms = key_terms + term
        out_ref[at, 2 * HD : 3 * HD] = raw
        out_ref[at, 3 * HD :] = grad_value.astype(LOW)
    spare = jnp.zeros((6, HD), F32)
    term_ref[...] = jnp.concatenate([query_terms, key_terms, spare], axis=0)
    one_ref[...] = sum_ref[...] + dot(out_ref[...], weight_ref[:, : 4 * HD], LAST)


BLOCK = D // 4


def iterate_kernel(*refs):
    pieces, out_ref, refs = refs[:8], refs[8], refs[9:]
    quarters, gram, high, low, poly, mixed_high, mixed_low, own, arrived = refs[:4], *refs[4:]
    copies = []
    for i in range(4):
        for part in range(2):
            place = [slice(None)] * 4
            place[(3 + i) % 4] = slice(part, part + 1)
            copies.append(
                pltpu.make_async_copy(
                    pieces[2 * i + part], quarters[i].at[tuple(place)], arrived.at[2 * i + part]
                )
            )
    for copy in copies:
        copy.start()
    for copy in copies:
        copy.wait()
    x0, x1, x2, x3 = [q.reshape(D, q.shape[-1]) for q in quarters]
    at = [slice(i * BLOCK, (i + 1) * BLOCK) for i in range(4)]
    blocks = [(i, j) for i in range(4) for j in range(4)]

    def parts(x):
        top = x.astype(LOW)
        return top, (x - top.astype(F32)).astype(LOW)

    def mirrored(ref, i, j, block):
        ref[at[i], at[j]] = block.astype(ref.dtype)
        if i != j:
            ref[at[j], at[i]] = block.T.astype(ref.dtype)

    def two_dot(left, right):
        rows = left.shape[0]
        both_parts = dot(jnp.concatenate(parts(left), axis=0), right)
        return both_parts[:rows] + both_parts[rows:]

    rows = lax.broadcasted_iota(jnp.int32, (BLOCK, BLOCK), 0)
    columns = lax.broadcasted_iota(jnp.int32, (BLOCK, BLOCK), 1)
    trace = jnp.zeros((1, 1), F32)
    for i, j in blocks:
        if j > i:
            continue
        block = sum(
            dot(x[at[i], : FF // 4], x[at[j], : FF // 4], LAST) for x in (x0, x1, x2, x3)
        )
        mirrored(gram, i, j, block)
        if i == j:
            diagonal = jnp.where(rows == columns, block, 0.0)
            trace = trace + jnp.sum(jnp.sum(diagonal, axis=1, keepdims=True), axis=0, keepdims=True)
    inverse = 1.0 / (jnp.sqrt(trace) + frob_eps)
    for i, j in blocks:
        block = gram[at[i], at[j]] * (inverse * inverse)
        gram[at[i], at[j]] = block
        high[at[i], at[j]], low[at[i], at[j]] = parts(block)
    own_rows = lax.broadcasted_iota(jnp.int32, own.shape, 0)
    own[...] = (own_rows == lax.broadcasted_iota(jnp.int32, own.shape, 1)).astype(F32)

    def set_poly():
        for i, j in blocks:
            if j > i:
                continue
            square = dot(high[at[i], :], high[:, at[j]])
            block = coef_square * high[at[i], at[j]].astype(F32) + coef_quartic * square
            mirrored(poly, i, j, block)

    def through_poly(x):
        return coef_linear * x + two_dot(x, poly[...])

    def sweep(_, carry):
        set_poly()
        own[...] = through_poly(own[...])
        for i, j in blocks:
            block = dot(high[at[i], :], poly[:, at[j]]) + dot(low[at[i], :], poly[:, at[j]])
            gram[at[i], at[j]] = (coef_linear * coef_linear) * gram[at[i], at[j]] + (
                2.0 * coef_linear
            ) * block
            mixed_high[at[i], at[j]], mixed_low[at[i], at[j]] = parts(block)
        for i, j in blocks:
            block = dot(mixed_high[at[i], :], poly[:, at[j]])
            block = block + dot(mixed_low[at[i], :], poly[:, at[j]]) + gram[at[i], at[j]]
            gram[at[i], at[j]] = block
            high[at[i], at[j]], low[at[i], at[j]] = parts(block)
        return carry

    lax.fori_loop(0, NS_ITERS - 2, sweep, 0)
    set_poly()
    own[...] = through_poly(own[...])

    def through_next(x):
        x = through_poly(x)
        x = two_dot(x, high[...]) + dot(x.astype(LOW), low[...])
        return through_poly(x)

    once = through_next(own[...])
    second = through_next(once)
    last = coef_linear * own[...] + coef_square * once + coef_quartic * second
    last = last * inverse
    for k, x in enumerate((x0, x1, x2, x3)):
        width = FF // 4
        out_ref[:, k * width : (k + 1) * width] = two_dot(last, x[:, :width]).astype(LOW)


def iterate_rows(pieces):
    square = pltpu.VMEM((D, D), LOW)
    quarters = [pltpu.VMEM((2, 2, 2, 2, D // 16, x.shape[-1]), LOW) for x in pieces[::2]]
    return pl.pallas_call(
        iterate_kernel,
        in_specs=[pl.BlockSpec(memory_space=pl.ANY)] * 8,
        out_specs=pl.BlockSpec(memory_space=pltpu.VMEM),
        out_shape=jax.ShapeDtypeStruct((64, FF), LOW),
        scratch_shapes=[
            *quarters,
            pltpu.VMEM((D, D), F32),
            *[square] * 5,
            pltpu.VMEM((64, D), F32),
            pltpu.SemaphoreType.DMA((8,)),
        ],
        compiler_params=pltpu.CompilerParams(vmem_limit_bytes=48 * 2**20),
        cost_estimate=pl.CostEstimate(flops=50 * 10**9, bytes_accessed=2**23, transcendentals=0),
    )(*pieces)


def by_sequence(width):
    return pl.BlockSpec((2 * SEQ, width), lambda s: (s, 0))


def whole(rows, width):
    return pl.BlockSpec((rows, width), lambda s: (0, 0))


SMALL = pl.CostEstimate(flops=2**20, bytes_accessed=2**16, transcendentals=0)
KERNEL_SPACE = pltpu.CompilerParams(vmem_limit_bytes=32 * 2**20)


def heads_forward(inputs, weight, cosine, sine, gain_rows, total):
    tokens = inputs.shape[0]
    return pl.pallas_call(
        heads_kernel,
        grid=(tokens // (2 * SEQ),),
        in_specs=[
            by_sequence(D),
            whole(D, 6 * HD),
            by_sequence(HD),
            by_sequence(HD),
            whole(8, HD),
            by_sequence(D),
        ],
        out_specs=[by_sequence(4 * HD), by_sequence(2 * HD), by_sequence(D)],
        out_shape=[
            jax.ShapeDtypeStruct((tokens, 4 * HD), F32),
            jax.ShapeDtypeStruct((tokens, 2 * HD), LOW),
            jax.ShapeDtypeStruct((tokens, D), F32),
        ],
        compiler_params=KERNEL_SPACE,
        cost_estimate=SMALL,
    )(inputs, weight, cosine, sine, gain_rows, total)


def heads_backward(raw, branch, weight, cosine, sine, gain_rows, total):
    tokens = raw.shape[0]
    grad_raw, terms, total = pl.pallas_call(
        heads_back_kernel,
        grid=(tokens // (2 * SEQ),),
        in_specs=[
            by_sequence(4 * HD),
            by_sequence(D),
            whole(D, 6 * HD),
            by_sequence(HD),
            by_sequence(HD),
            whole(8, HD),
            by_sequence(D),
        ],
        out_specs=[
            by_sequence(4 * HD),
            pl.BlockSpec((8, HD), lambda s: (s, 0)),
            by_sequence(D),
        ],
        out_shape=[
            jax.ShapeDtypeStruct((tokens, 4 * HD), LOW),
            jax.ShapeDtypeStruct((tokens // (2 * SEQ) * 8, HD), F32),
            jax.ShapeDtypeStruct((tokens, D), F32),
        ],
        scratch_shapes=[pltpu.VMEM((2 * SEQ, 2 * HD), LOW)],
        compiler_params=KERNEL_SPACE,
        cost_estimate=SMALL,
    )(raw, branch, weight, cosine, sine, gain_rows, total)
    return grad_raw, jnp.sum(terms.reshape(-1, 8, HD), axis=0), total


def inner_kernel(
    input_ref, grad_ref, w0, w1, w2, w3, act_ref, inner_ref, outward_ref, back_ref
):
    width = FF // 8
    outward, back = 0.0, 0.0
    for i, w in enumerate((w0, w1, w2, w3)):
        gate_up = dot(input_ref[...], w[:, : 2 * width])
        gate, up = gate_up[:, :width], gate_up[:, width:]
        sigmoid = jax.nn.sigmoid(gate)
        swish = gate * sigmoid
        act = (swish * up).astype(LOW)
        act_ref[:, i * width : (i + 1) * width] = act
        grad_act = dot(grad_ref[...], w[:, 2 * width :])
        slope = sigmoid * (1.0 + gate * (1.0 - sigmoid))
        start = i * 2 * width
        inner_ref[:, start : start + width] = (grad_act * up * slope).astype(LOW)
        inner_ref[:, start + width : start + 2 * width] = (grad_act * swish).astype(LOW)
        outward = outward + dot(act, w[:, 2 * width :], LAST)
        back = back + dot(inner_ref[:, start : start + 2 * width], w[:, : 2 * width], LAST)
    outward_ref[...] = outward
    back_ref[...] = back


def inner_units(inputs, grads, weights):
    tokens = inputs.shape[0]
    return pl.pallas_call(
        inner_kernel,
        in_specs=[pl.BlockSpec(memory_space=pltpu.VMEM)] * 6,
        out_specs=[pl.BlockSpec(memory_space=pltpu.VMEM)] * 4,
        out_shape=[
            jax.ShapeDtypeStruct((tokens, FF // 2), LOW),
            jax.ShapeDtypeStruct((tokens, FF), LOW),
            jax.ShapeDtypeStruct((tokens, D), F32),
            jax.ShapeDtypeStruct((tokens, D), F32),
        ],
        compiler_params=pltpu.CompilerParams(vmem_limit_bytes=48 * 2**20),
        cost_estimate=SMALL,
    )(inputs, grads, *weights)


def terms_kernel(link, first_left, first_right, second_left, second_right, kept_ref, sent_ref):
    width = first_right.shape[1]
    first = dot(first_left[...], first_right[...], ROWS).astype(LOW)
    second = dot(second_left[...], second_right[...], ROWS).astype(LOW)

    def put(ref, to, start, rows):
        ref[to : to + rows, :width] = first[start : start + rows]
        ref[to : to + rows, width:] = second[start : start + rows]

    if link < 2:
        block = pl.program_id(0)
        part = block // 2 if link == 0 else block % 2

        @pl.when(part == 0)
        def _():
            put(kept_ref, 0, 0, BLOCK)

        @pl.when(part == 1)
        def _():
            put(sent_ref, 0, 0, BLOCK)

    else:
        rows = 128 if link == 2 else 64
        for start in range(0, BLOCK, 2 * rows):
            put(kept_ref, start // 2, start, rows)
            put(sent_ref, start // 2, start + rows, rows)


def terms(link, first_left, first_right, second_left, second_right):
    tokens = first_left.shape[0]

    def right(x, at, width):
        return x, pl.BlockSpec((tokens, width), lambda r: (0, at))

    left = pl.BlockSpec((tokens, BLOCK), lambda r: (0, r))
    operands = [(first_left, left), right(*first_right), (second_left, left), right(*second_right)]
    width = first_right[2] + second_right[2]
    if link == 0:
        specs = [
            pl.BlockSpec((BLOCK, width), lambda r: (jnp.minimum(r, 1), 0)),
            pl.BlockSpec((BLOCK, width), lambda r: (jnp.maximum(r - 2, 0), 0)),
        ]
    elif link == 1:
        specs = [pl.BlockSpec((BLOCK, width), lambda r: (r // 2, 0))] * 2
    else:
        specs = [pl.BlockSpec((BLOCK // 2, width), lambda r: (r, 0))] * 2
    half = jax.ShapeDtypeStruct((D // 2, width), LOW)
    kept, sent = pl.pallas_call(
        functools.partial(terms_kernel, link),
        grid=(4,),
        in_specs=[spec for _, spec in operands],
        out_specs=specs,
        out_shape=[half, half],
        compiler_params=KERNEL_SPACE,
        cost_estimate=SMALL,
    )(*[x for x, _ in operands])
    shape = [2, 2, 2, 2, D // 16, width]
    shape[link] = 1
    return kept.reshape(shape), sent.reshape(shape)


def shared_sum(partial):
    own = partial.shape[0] // 2
    return partial[:own] + swap(partial[own:].astype(LOW)).astype(F32)


def both(x):
    return jnp.concatenate([x, swap(x)], axis=0)


def norm_back(grad_hat, normed, scale):
    return scale * (grad_hat - normed * jnp.mean(grad_hat * normed, axis=-1, keepdims=True))


HEADS_WIDTH, INNER_WIDTH = 6 * HD, 3 * FF // 8


def pieces_of(core):
    pieces = []
    for i in range(core * 4, core * 4 + 4):
        pieces += [(0, i * 2 * HD, 2 * HD), (1, i * HD, HD), (2, i * HD, HD), (3, i * 2 * HD, 2 * HD)]
    for i in range(core * 4, core * 4 + 4):
        pieces += [(m, i * FF // 8, FF // 8) for m in (4, 5, 6)]
    return pieces


HALF_WIDTH = sum(WIDTHS) // 2


def compact_kernel(at_ref, top_ref, low_ref, mine_ref, theirs_ref):
    for core in range(2):

        @pl.when(at_ref[7] == core)
        def _():
            for out_ref, pieces in ((mine_ref, pieces_of(core)), (theirs_ref, pieces_of(1 - core))):
                to = 0
                for m, start, width in pieces:
                    out_ref[:16, to : to + width] = top_ref[at_ref[m], :, start : start + width]
                    out_ref[16:, to : to + width] = low_ref[at_ref[m], :, start : start + width]
                    to += width


def compact(at, top, low):
    half = jax.ShapeDtypeStruct((32, HALF_WIDTH), LOW)
    in_vmem = pl.BlockSpec(memory_space=pltpu.VMEM)
    return pl.pallas_call(
        compact_kernel,
        in_specs=[pl.BlockSpec(memory_space=pltpu.SMEM), in_vmem, in_vmem],
        out_specs=[in_vmem, in_vmem],
        out_shape=[half, half],
        compiler_params=pltpu.CompilerParams(vmem_limit_bytes=24 * 2**20),
        cost_estimate=pl.CostEstimate(flops=0, bytes_accessed=5 * 2**20, transcendentals=0),
    )(at, top, low)


def route_kernel(of_ref, kept_ref, got_ref, top_keep, top_send, low_keep, low_send, held):
    held[...] = jnp.zeros_like(held)
    for core in range(2):

        @pl.when(of_ref[8] == core)
        def _():
            for in_ref, pieces in ((kept_ref, pieces_of(core)), (got_ref, pieces_of(1 - core))):
                at = 0
                for m, start, width in pieces:
                    held[m, :, start : start + width] = in_ref[:, at : at + width]
                    at += width

    for place in range(8):
        near, far, j = place // 4, (place // 2) % 2, place % 2
        (top_keep, top_send)[near][2 * far + j] = held[of_ref[place], :16, :]
        (low_keep, low_send)[far][2 * near + j] = held[of_ref[place], 16:, :]


def route(of, kept, got):
    half = jax.ShapeDtypeStruct((4, 16, FF), LOW)
    in_vmem = pl.BlockSpec(memory_space=pltpu.VMEM)
    return pl.pallas_call(
        route_kernel,
        in_specs=[pl.BlockSpec(memory_space=pltpu.SMEM), in_vmem, in_vmem],
        out_specs=[in_vmem] * 4,
        out_shape=[half] * 4,
        scratch_shapes=[pltpu.VMEM((8, 32, FF), LOW)],
        compiler_params=pltpu.CompilerParams(vmem_limit_bytes=24 * 2**20),
        cost_estimate=pl.CostEstimate(flops=0, bytes_accessed=5 * 2**20, transcendentals=0),
    )(of, kept, got)


def shards(
    hidden_in,
    out_grad,
    seq_owner,
    token_place,
    matrix_slot,
    weight_slots,
    momentum_slots,
    gains,
    gain_momentum,
):
    slot_count, length = hidden_in.shape[:2]
    tok_count = slot_count * length
    z, y = lax.axis_index("dp_0"), lax.axis_index("dp_1")
    core, group = lax.axis_index("dp_2"), lax.axis_index("group")
    first_core = core == 0
    replica = ((z * 4 + y) * 2 + core) * 4 + group

    def core_pick(zero, one):
        return jnp.where(first_core, zero, one)

    weight_low = weight_slots.astype(LOW)
    (slots_top, slots_low), hidden_in = gather_group(
        [weight_low[:, :16], weight_low[:, 16:]], hidden_in
    )
    at = place_of(jnp.bitwise_xor(group, matrix_slot >> 1)) * 2 + (matrix_slot & 1)
    mine, theirs = compact(jnp.concatenate([at, core[None]]), slots_top, slots_low)
    got = swap(theirs)
    chip_rows = core_pick(
        jnp.concatenate([mine, got], axis=0), jnp.concatenate([got, mine], axis=0)
    )
    heads_held = gather_shaped(chip_rows[:, : 4 * HEADS_WIDTH], HEADS_WIDTH)
    inner_held = gather_shaped(chip_rows[:, 4 * HEADS_WIDTH :], INNER_WIDTH)
    column = lax.broadcasted_iota(jnp.int32, (D, D), 1)
    source = lax.broadcasted_iota(jnp.int32, (D, D), 0)
    block = column // 64
    near_z, near_y = block // 8, (block // 4) % 2
    far_z, far_y = (block // 2) % 2, block % 2
    from_z = jnp.bitwise_xor(z, jnp.bitwise_xor(near_z, far_z * 3))
    from_y = jnp.bitwise_xor(y, jnp.bitwise_xor(near_y, far_y * 3))
    reorder = (source == (from_z * 4 + from_y) * 64 + column % 64).astype(LOW)

    live_count = jnp.sum((seq_owner == replica).astype(jnp.int32))
    live_slot = (jnp.arange(slot_count, dtype=jnp.int32) < live_count).astype(F32)
    live_token = jnp.repeat(live_slot, length)[:, None]
    tokens = dot(hidden_in.reshape(tok_count, D), reorder)
    grad_out = dot(out_grad.reshape(tok_count, D), reorder) * live_token
    grad_low = both(grad_out.astype(LOW))
    layer_gains = jnp.dot(
        gains[: 2 * D].reshape(2, D), reorder.astype(F32), precision=lax.Precision.HIGHEST
    )
    gain_one, gain_two = layer_gains[0:1], layer_gains[1:2]
    gain_rows = jnp.pad(gains[2 * D :].reshape(2, HD), ((0, 6), (0, 0)))
    places = both(token_place).astype(F32).reshape(-1, 1)
    exponent = jnp.arange(HD // 2, dtype=F32) * (-2.0 / HD)
    angles = places * jnp.power(rope_base, exponent)[None, :]
    cosine, sine = jnp.cos(angles), jnp.sin(angles)
    cosine = jnp.concatenate([cosine, cosine], axis=1)
    sine = jnp.concatenate([-sine, sine], axis=1)

    scale_one = lax.rsqrt(jnp.mean(tokens * tokens, axis=-1, keepdims=True) + norm_eps)
    normed_one = tokens * scale_one
    input_one = both((normed_one * gain_one).astype(LOW))
    heads_held = together(gather_step(heads_held, 0))
    held = together([*gather_step(heads_held, 1), *gather_step(inner_held, 0)])
    held = together([*gather_step(held[:4], 2), *gather_step(held[4:], 1)])
    held = together([*gather_step(held[:4], 3), *gather_step(held[4:], 2)])
    w_heads = flat(held[:4])
    w_inner = flat(gather_step(held[4:], 3))
    raw, attn = [], []
    branch = jnp.zeros((2 * tok_count, D), F32)
    for w in w_heads:
        fresh, heads, branch = heads_forward(input_one, w, cosine, sine, gain_rows, branch)
        raw.append(fresh)
        attn.append(heads)
    *w_inner, branch = together([*w_inner, branch])
    residual = tokens + shared_sum(branch)
    scale_two = lax.rsqrt(jnp.mean(residual * residual, axis=-1, keepdims=True) + norm_eps)
    normed_two = residual * scale_two
    input_two = both((normed_two * gain_two).astype(LOW))
    act, grad_inner, outward, grad_two = inner_units(input_two, grad_low, w_inner)
    result = (residual + shared_sum(outward)) * live_token
    hidden_out = dot(result.astype(LOW), reorder, LAST).astype(LOW)

    sent, kept = [], []
    for i in range(4):
        keep, send = terms(
            i, input_two, (grad_inner, i, FF // 4), grad_low, (act, i, FF // 8)
        )
        sent.append(send)
        kept.append(keep)
    grad_two = shared_sum(grad_two)
    gain_two_term = jnp.sum(grad_two * normed_two, axis=0, keepdims=True)
    grad_residual = grad_out + norm_back(grad_two * gain_two, normed_two, scale_two)
    branch_low = both(grad_residual.astype(LOW))
    grad_one, head_terms, grad_raw = jnp.zeros((2 * tok_count, D), F32), 0.0, []
    heads_sent, heads_kept = [], []

    def back_through(i, branch, grad_one):
        fresh, term, grad_one = heads_backward(
            raw[i], branch, w_heads[i], cosine, sine, gain_rows, grad_one
        )
        grad_raw.append(fresh)
        return head_terms + term, grad_one

    def heads_terms(i):
        keep, send = terms(
            i, input_one, (grad_raw[i], 0, 4 * HD), branch_low, (attn[i], 0, 2 * HD)
        )
        heads_kept.append(keep)
        heads_sent.append(send)

    head_terms, grad_one = back_through(0, branch_low, grad_one)
    head_terms, grad_one = back_through(1, branch_low, grad_one)
    sent, kept = scatter_step(sent, kept, 0)
    *held, branch_low, grad_one = together([*sent, *kept, branch_low, grad_one])
    sent, kept = held[:4], held[4:]
    head_terms, grad_one = back_through(2, branch_low, grad_one)
    heads_terms(0)
    sent, kept = scatter_step(sent, kept, 1)
    *held, branch_low, heads_sent[0], grad_one = together(
        [*sent, *kept, branch_low, heads_sent[0], grad_one]
    )
    sent, kept = held[:4], held[4:]
    head_terms, grad_one = back_through(3, branch_low, grad_one)
    heads_terms(1)
    sent, kept = scatter_step(sent, kept, 2)
    *held, heads_sent[1], grad_one = together([*sent, *kept, heads_sent[1], grad_one])
    sent, kept = held[:4], held[4:]
    heads_terms(2)
    heads_terms(3)
    sent, kept = scatter_step(sent, kept, 3)
    inner_sums = flat(kept)
    sent, kept = heads_sent, heads_kept
    grad_one = shared_sum(grad_one)
    gain_one_term = jnp.sum(grad_one * normed_one, axis=0, keepdims=True)
    in_grad = grad_residual + norm_back(grad_one * gain_one, normed_one, scale_one)
    in_high, in_low = split_two(in_grad)
    in_grad = dot(in_high, reorder, LAST) + dot(in_low, reorder, LAST)
    layer_terms = lax.dot_general(
        jnp.concatenate([gain_one_term, gain_two_term], axis=0),
        reorder.astype(F32),
        (LAST, ((), ())),
        precision=lax.Precision.HIGHEST,
    )
    gain_sum = jnp.concatenate([layer_terms.reshape(-1), head_terms[:2].reshape(-1)])
    for step in range(4):
        sent, kept = scatter_step(sent, kept, step)
        if step == 1:
            gain_sum = gain_sum + swap(gain_sum)
        elif step > 1:
            gain_sum = gain_sum + lax.ppermute(gain_sum, "group", (NEAR, FAR)[step - 2])
        if step == 0:
            *held, in_grad, gain_sum = together([*sent, *kept, in_grad, gain_sum])
        else:
            *held, gain_sum = together([*sent, *kept, gain_sum])
        sent, kept = held[:-4], held[-4:]
    heads_sums = flat(kept)

    sums = jnp.concatenate([*heads_sums, *inner_sums], axis=1)
    kept = core_pick(sums[:32], sums[32:])
    got = swap(core_pick(sums[32:], sums[:32]))
    slot_at = (jnp.bitwise_xor(group, jnp.asarray(MASKS, jnp.int32)) * 2)[:, None]
    slot_at = (slot_at + jnp.arange(2, dtype=jnp.int32)[None, :]).reshape(8)
    matches = slot_at[:, None] == matrix_slot[None, :]
    numbers = jnp.arange(7, dtype=jnp.int32)[None, :]
    routed_from = 7 - jnp.max(jnp.where(matches, 7 - numbers, 0), axis=1)
    halves = route(jnp.concatenate([routed_from, core[None]]), kept, got)
    sent, kept = [halves[1], halves[3]], [halves[0], halves[2]]
    for step in range(2):
        got = together(
            [lax.ppermute(sent[i], "group", (NEAR, FAR)[(step + i) % 2]) for i in range(2)]
        )
        total = [kept[i].astype(F32) + got[i].astype(F32) for i in range(2)]
        if step == 0:
            held = together([*(t[2:].astype(LOW) for t in total), *(t[:2].astype(LOW) for t in total)])
            sent, kept = held[:2], held[2:]
    weight_grad = jnp.concatenate(total, axis=1)

    own_ids = group * 2 + jnp.arange(2, dtype=jnp.int32)
    own_match = own_ids[:, None] == matrix_slot[None, :]
    own_width = jnp.sum(jnp.where(own_match, jnp.asarray(WIDTHS, jnp.int32)[None, :], 0), axis=1)
    own_width = own_width.astype(jnp.int32)
    column_mask = (jnp.arange(FF, dtype=jnp.int32)[None, :] < own_width[:, None]).astype(F32)
    column_mask = column_mask[:, None, :]
    momentum_new = column_mask * (momentum_keep * momentum_slots + weight_grad)
    direction = (weight_grad + momentum_keep * momentum_new).astype(LOW)

    mine = core_pick(direction[0], direction[1])
    got = swap(core_pick(direction[1], direction[0]))
    rows = core_pick(jnp.concatenate([mine, got], axis=0), jnp.concatenate([got, mine], axis=0))
    gain_parts, rest = [], gain_sum
    for _ in range(3):
        part = lax.reduce_precision(rest, exponent_bits=8, mantissa_bits=7)
        gain_parts.append(part.astype(LOW))
        rest = rest - part
    gain_parts = jnp.pad(jnp.concatenate(gain_parts), (0, 64 * HD - 3 * gain_sum.shape[0]))
    held = gather_shaped(rows, FF // 4)
    held[0] = jnp.concatenate([held[0], gain_parts.reshape(1, 1, 1, 1, 64, HD)], axis=-1)
    for step in range(3):
        held = together(gather_step(held, step))
    fresh = gather_came(held, 3)
    pieces = [x for pair in zip(held, fresh) for x in pair]
    gain_parts = jnp.concatenate([x[..., FF // 4 :] for x in pieces[:2]], axis=3)
    gain_parts = gain_parts.reshape(16, 64 * HD)
    place = lax.broadcasted_iota(jnp.int32, (16, 16), 1)
    of_z = jnp.bitwise_xor(z, jnp.bitwise_xor(place // 8, (place // 2) % 2 * 3))
    of_y = jnp.bitwise_xor(y, jnp.bitwise_xor((place // 4) % 2, place % 2 * 3))
    in_turn = (lax.broadcasted_iota(jnp.int32, (16, 16), 0) == of_z * 4 + of_y).astype(LOW)
    gain_parts = dot(in_turn, gain_parts)[:, : 3 * gain_sum.shape[0]].reshape(16, 3, -1)
    gain_grad = jnp.sum(gain_parts[:, 0] + gain_parts[:, 1] + gain_parts[:, 2], axis=0)
    iterate = iterate_rows(pieces)
    kept = core_pick(iterate[:32], iterate[32:])
    got = swap(core_pick(iterate[32:], iterate[:32]))
    iterate = jnp.stack([core_pick(kept, got), core_pick(got, kept)]).astype(F32)
    update_scale = 0.2 * jnp.sqrt(jnp.maximum(own_width, D).astype(F32))
    weight_new = column_mask * (
        weight_slots * (1.0 - learn_rate * weight_decay)
        - learn_rate * update_scale[:, None, None] * iterate
    )

    gain_momentum_new = momentum_keep * gain_momentum + gain_grad
    gain_step = gain_grad + momentum_keep * gain_momentum_new
    bounds = (0, D, 2 * D, 2 * D + HD, 2 * D + 2 * HD)
    scaled_parts = []
    for number in range(4):
        segment = gain_step[bounds[number] : bounds[number + 1]]
        scaled_parts.append(segment * lax.rsqrt(jnp.mean(segment * segment) + norm_eps))
    gain_new = gains - gain_rate * jnp.concatenate(scaled_parts)
    shape = (slot_count, length, D)
    return (
        hidden_out.reshape(shape),
        in_grad.reshape(shape),
        weight_grad,
        momentum_new,
        weight_new,
        gain_grad,
        gain_momentum_new,
        gain_new,
    )


def solution(mesh):
    finer = Mesh(
        mesh.devices.reshape(4, 4, 2, mesh.shape["group"]), ("dp_0", "dp_1", "dp_2", "group")
    )
    in_specs = (
        P(DP_GROUP, None, None),
        P(DP_GROUP, None, None),
        P(),
        P(DP_GROUP, None),
        P(),
        P("group", ("dp_0", "dp_1", "dp_2"), None),
        P("group", ("dp_0", "dp_1", "dp_2"), None),
        P(),
        P(),
    )
    out_specs = (
        P(DP_GROUP, None, None),
        P(DP_GROUP, None, None),
        P("group", ("dp_0", "dp_1", "dp_2"), None),
        P("group", ("dp_0", "dp_1", "dp_2"), None),
        P("group", ("dp_0", "dp_1", "dp_2"), None),
        P(),
        P(),
        P(),
    )
    return jax.shard_map(
        shards, mesh=finer, in_specs=in_specs, out_specs=out_specs, check_vma=False
    )
```

```python
import functools

import jax
import jax.numpy as jnp
from jax import lax
from jax.experimental import pallas as pl
from jax.experimental.pallas import tpu as pltpu
from jax.sharding import Mesh
from jax.sharding import PartitionSpec as P

D = 1024
HEADS = 16
KV = 8
HD = 128
FF = 3072
SEQ = 128
NS_ITERS = 5
WIDTHS = (HEADS * HD, KV * HD, KV * HD, HEADS * HD, FF, FF, FF)
DP_GROUP = ("dp_0", "dp_1", "dp_2", "group")
LOW = jnp.bfloat16
F32 = jnp.float32

norm_eps = 1e-06
frob_eps = 1e-07
rope_base = 1000000.0
coef_linear = 3.4445
coef_square = -4.775
coef_quartic = 2.0315
momentum_keep = 0.95
learn_rate = 0.15
weight_decay = 0.1
gain_rate = 0.5
masked_score = -1e30
score_scale = HD ** (-0.5)

NEAR = ((0, 1), (1, 0), (2, 3), (3, 2))
FAR = ((0, 3), (3, 0), (1, 2), (2, 1))
LINKS = (("dp_0", NEAR), ("dp_1", NEAR), ("dp_0", FAR), ("dp_1", FAR))
MASKS = (0, 3, 1, 2)


def place_of(mask):
    return jnp.where(mask == 0, 0, jnp.where(mask == 3, 1, mask + 1))


def swap(x):
    return lax.ppermute(x, "dp_2", ((0, 1), (1, 0)))


def together(arrays):
    return list(lax.optimization_barrier(tuple(arrays)))


def gather_came(quarters, step):
    fresh = []
    for i in range(4):
        axis, pairs = LINKS[(step + i) % 4]
        fresh.append(lax.ppermute(quarters[i], axis, pairs))
    return together(fresh)


def gather_step(quarters, step):
    fresh = gather_came(quarters, step)
    return [
        jnp.concatenate([quarters[i], fresh[i]], axis=(step + i) % 4) for i in range(4)
    ]


def gather_shaped(x, width):
    return [
        x[:, i * width : (i + 1) * width].reshape(1, 1, 1, 1, x.shape[0], width) for i in range(4)
    ]


def flat(quarters):
    return [q.reshape(-1, q.shape[-1]) for q in quarters]


def scatter_step(sent, kept, step):
    to_send, to_keep, came = [], [], []
    for i in range(4):
        axis, pairs = LINKS[(step + i) % 4]
        came.append(lax.ppermute(sent[i], axis, pairs))
    came = together(came)
    for i in range(4):
        at = (step + 1 + i) % 4

        def half(part):
            if step == 3:
                return (kept[i].astype(F32) + came[i].astype(F32)).astype(LOW)
            both_parts = [lax.slice_in_dim(x, part, part + 1, axis=at) for x in (kept[i], came[i])]
            return (both_parts[0].astype(F32) + both_parts[1].astype(F32)).astype(LOW)

        to_keep.append(half(0))
        if step < 3:
            to_send.append(half(1))
    return to_send, to_keep


def gather_group(halves, after):
    held = [h[None, None] for h in halves]
    for step in range(2):
        fresh = [lax.ppermute(held[i], "group", (NEAR, FAR)[(step + i) % 2]) for i in range(2)]
        if step == 0:
            *fresh, after = together([*fresh, after])
        held = [jnp.concatenate([held[i], fresh[i]], axis=(step + i) % 2) for i in range(2)]
    return [h.reshape(8, *h.shape[3:]) for h in held], after


def dot(left, right, dims=((1,), (0,))):
    return lax.dot_general(left, right, (dims, ((), ())), preferred_element_type=F32)


ROWS = ((0,), (0,))
LAST = ((1,), (1,))
PLAIN = ((1,), (0,))


def split_two(x):
    high = lax.reduce_precision(x, exponent_bits=8, mantissa_bits=7)
    return high.astype(LOW), (x - high).astype(LOW)


def half_turn(u):
    return jnp.concatenate([u[:, HD // 2 :], u[:, : HD // 2]], axis=1)


def fetch(pieces, quarter, arrived, link):
    copies = []
    for part in range(2):
        place = [slice(None)] * 4
        place[link] = slice(part, part + 1)
        copies.append(
            pltpu.make_async_copy(pieces[part], quarter.at[tuple(place)], arrived.at[part])
        )
    return copies


def head_forward(raw, gain, cosine, sine):
    scale = lax.rsqrt(jnp.mean(raw * raw, axis=-1, keepdims=True) + norm_eps)
    normed = raw * scale
    gained = normed * gain
    turned = gained * cosine + half_turn(gained) * sine
    return normed, scale, turned.astype(LOW)


def softmax_parts(query, key):
    scores = dot(query, key, LAST) * score_scale
    rows = lax.broadcasted_iota(jnp.int32, scores.shape, 0) & (SEQ - 1)
    columns = lax.broadcasted_iota(jnp.int32, scores.shape, 1)
    scores = jnp.where(rows >= columns, scores, masked_score)
    terms = jnp.exp(scores - jnp.max(scores, axis=-1, keepdims=True))
    return terms / jnp.sum(terms, axis=-1, keepdims=True)


def two_heads(ref, at):
    return jnp.concatenate([ref[at, :HD], ref[at, HD : 2 * HD]], axis=0)


def twice(x):
    return jnp.concatenate([x, x], axis=0)


def heads_kernel(
    link,
    input_ref,
    held_ref,
    fresh_ref,
    cos_ref,
    sin_ref,
    gain_ref,
    sum_ref,
    raw_ref,
    attn_ref,
    out_ref,
    quarter,
    arrived,
):
    @pl.when(pl.program_id(0) == 0)
    def _():
        copies = fetch((held_ref, fresh_ref), quarter, arrived, link)
        for copy in copies:
            copy.start()
        for copy in copies:
            copy.wait()

    weight_ref = quarter.reshape(D, HEADS_WIDTH)
    raw_ref[...] = dot(input_ref[...], weight_ref[:, : 4 * HD])
    for b in range(raw_ref.shape[0] // SEQ):
        at = slice(b * SEQ, (b + 1) * SEQ)
        cosine, sine = cos_ref[at, :], sin_ref[at, :]
        _, _, key = head_forward(raw_ref[at, 2 * HD : 3 * HD], gain_ref[1:2, :], cosine, sine)
        value = raw_ref[at, 3 * HD :].astype(LOW)
        _, _, query = head_forward(
            two_heads(raw_ref, at), gain_ref[0:1, :], twice(cosine), twice(sine)
        )
        probs = softmax_parts(query, key).astype(LOW)
        out = dot(probs, value).astype(LOW)
        attn_ref[at, :HD] = out[:SEQ]
        attn_ref[at, HD:] = out[SEQ:]
    out_ref[...] = sum_ref[...] + dot(attn_ref[...], weight_ref[:, 4 * HD :], LAST)


def head_backward(grad, normed, scale, gain, cosine, sine):
    back = grad * cosine - half_turn(grad) * sine
    term = jnp.sum(back * normed, axis=0, keepdims=True)
    g = back * gain
    raw = scale * (g - normed * jnp.mean(g * normed, axis=-1, keepdims=True))
    return raw.astype(LOW), term


def heads_back_kernel(
    link,
    raw_ref,
    branch_ref,
    held_ref,
    fresh_ref,
    cos_ref,
    sin_ref,
    gain_ref,
    sum_ref,
    out_ref,
    term_ref,
    one_ref,
    grad_ref,
    quarter,
    arrived,
):
    @pl.when(pl.program_id(0) == 0)
    def _():
        copies = fetch((held_ref, fresh_ref), quarter, arrived, link)
        for copy in copies:
            copy.start()
        for copy in copies:
            copy.wait()

    weight_ref = quarter.reshape(D, HEADS_WIDTH)
    grad_ref[...] = dot(branch_ref[...], weight_ref[:, 4 * HD :]).astype(LOW)
    query_terms, key_terms = 0.0, 0.0
    for b in range(raw_ref.shape[0] // SEQ):
        at = slice(b * SEQ, (b + 1) * SEQ)
        cosine, sine = cos_ref[at, :], sin_ref[at, :]
        cosines, sines = twice(cosine), twice(sine)
        key_hat, key_scale, key = head_forward(
            raw_ref[at, 2 * HD : 3 * HD], gain_ref[1:2, :], cosine, sine
        )
        value = raw_ref[at, 3 * HD :].astype(LOW)
        query_hat, query_scale, query = head_forward(
            two_heads(raw_ref, at), gain_ref[0:1, :], cosines, sines
        )
        probs = softmax_parts(query, key)
        grad_attn = two_heads(grad_ref, at)
        grad_value = dot(probs.astype(LOW), grad_attn, ROWS)
        grad_probs = dot(grad_attn, value, LAST)
        inner = jnp.sum(probs * grad_probs, axis=-1, keepdims=True)
        grad_scores = (probs * (grad_probs - inner)).astype(LOW)
        grad_query = dot(grad_scores, key) * score_scale
        grad_key = dot(grad_scores, query, ROWS) * score_scale
        raw, term = head_backward(
            grad_query, query_hat, query_scale, gain_ref[0:1, :], cosines, sines
        )
        query_terms = query_terms + term
        out_ref[at, :HD] = raw[:SEQ]
        out_ref[at, HD : 2 * HD] = raw[SEQ:]
        raw, term = head_backward(grad_key, key_hat, key_scale, gain_ref[1:2, :], cosine, sine)
        key_terms = key_terms + term
        out_ref[at, 2 * HD : 3 * HD] = raw
        out_ref[at, 3 * HD :] = grad_value.astype(LOW)
    spare = jnp.zeros((6, HD), F32)
    term_ref[...] = jnp.concatenate([query_terms, key_terms, spare], axis=0)
    one_ref[...] = sum_ref[...] + dot(out_ref[...], weight_ref[:, : 4 * HD], LAST)


BLOCK = D // 4


def iterate_kernel(*refs):
    pieces, out_ref, refs = refs[:8], refs[8], refs[9:]
    quarters, gram, high, low, poly, mixed_high, mixed_low, own, arrived = refs[:4], *refs[4:]
    copies = [
        copy
        for i in range(4)
        for copy in fetch(pieces[2 * i : 2 * i + 2], quarters[i], arrived.at[i], (3 + i) % 4)
    ]
    for copy in copies:
        copy.start()
    for copy in copies:
        copy.wait()
    x0, x1, x2, x3 = [q.reshape(D, q.shape[-1]) for q in quarters]
    at = [slice(i * BLOCK, (i + 1) * BLOCK) for i in range(4)]
    blocks = [(i, j) for i in range(4) for j in range(4)]

    def parts(x):
        top = x.astype(LOW)
        return top, (x - top.astype(F32)).astype(LOW)

    def mirrored(ref, i, j, block):
        ref[at[i], at[j]] = block.astype(ref.dtype)
        if i != j:
            ref[at[j], at[i]] = block.T.astype(ref.dtype)

    def two_dot(left, right):
        rows = left.shape[0]
        both_parts = dot(jnp.concatenate(parts(left), axis=0), right)
        return both_parts[:rows] + both_parts[rows:]

    rows = lax.broadcasted_iota(jnp.int32, (BLOCK, BLOCK), 0)
    columns = lax.broadcasted_iota(jnp.int32, (BLOCK, BLOCK), 1)
    trace = jnp.zeros((1, 1), F32)
    for i, j in blocks:
        if j > i:
            continue
        block = sum(
            dot(x[at[i], : FF // 4], x[at[j], : FF // 4], LAST) for x in (x0, x1, x2, x3)
        )
        mirrored(gram, i, j, block)
        if i == j:
            diagonal = jnp.where(rows == columns, block, 0.0)
            trace = trace + jnp.sum(jnp.sum(diagonal, axis=1, keepdims=True), axis=0, keepdims=True)
    inverse = 1.0 / (jnp.sqrt(trace) + frob_eps)
    for i, j in blocks:
        block = gram[at[i], at[j]] * (inverse * inverse)
        gram[at[i], at[j]] = block
        high[at[i], at[j]], low[at[i], at[j]] = parts(block)
    own_rows = lax.broadcasted_iota(jnp.int32, own.shape, 0)
    own[...] = (own_rows == lax.broadcasted_iota(jnp.int32, own.shape, 1)).astype(F32)

    def set_poly():
        for i, j in blocks:
            if j > i:
                continue
            square = dot(high[at[i], :], high[:, at[j]])
            block = coef_square * high[at[i], at[j]].astype(F32) + coef_quartic * square
            mirrored(poly, i, j, block)

    def through_poly(x):
        return coef_linear * x + two_dot(x, poly[...])

    def sweep(_, carry):
        set_poly()
        own[...] = through_poly(own[...])
        for i, j in blocks:
            block = dot(high[at[i], :], poly[:, at[j]]) + dot(low[at[i], :], poly[:, at[j]])
            gram[at[i], at[j]] = (coef_linear * coef_linear) * gram[at[i], at[j]] + (
                2.0 * coef_linear
            ) * block
            mixed_high[at[i], at[j]], mixed_low[at[i], at[j]] = parts(block)
        for i, j in blocks:
            block = dot(mixed_high[at[i], :], poly[:, at[j]])
            block = block + dot(mixed_low[at[i], :], poly[:, at[j]]) + gram[at[i], at[j]]
            gram[at[i], at[j]] = block
            high[at[i], at[j]], low[at[i], at[j]] = parts(block)
        return carry

    lax.fori_loop(0, NS_ITERS - 2, sweep, 0)
    set_poly()
    own[...] = through_poly(own[...])

    def through_next(x):
        x = through_poly(x)
        x = two_dot(x, high[...]) + dot(x.astype(LOW), low[...])
        return through_poly(x)

    once = through_next(own[...])
    second = through_next(once)
    last = coef_linear * own[...] + coef_square * once + coef_quartic * second
    last = last * inverse
    for k, x in enumerate((x0, x1, x2, x3)):
        width = FF // 4
        out_ref[:, k * width : (k + 1) * width] = two_dot(last, x[:, :width]).astype(LOW)


def iterate_rows(pieces):
    square = pltpu.VMEM((D, D), LOW)
    quarters = [pltpu.VMEM((2, 2, 2, 2, D // 16, x.shape[-1]), LOW) for x in pieces[::2]]
    return pl.pallas_call(
        iterate_kernel,
        in_specs=[pl.BlockSpec(memory_space=pl.ANY)] * 8,
        out_specs=pl.BlockSpec(memory_space=pltpu.VMEM),
        out_shape=jax.ShapeDtypeStruct((64, FF), LOW),
        scratch_shapes=[
            *quarters,
            pltpu.VMEM((D, D), F32),
            *[square] * 5,
            pltpu.VMEM((64, D), F32),
            pltpu.SemaphoreType.DMA((4, 2)),
        ],
        compiler_params=pltpu.CompilerParams(vmem_limit_bytes=32 * 2**20),
        cost_estimate=pl.CostEstimate(flops=50 * 10**9, bytes_accessed=2**23, transcendentals=0),
    )(*pieces)


def by_sequence(width):
    return pl.BlockSpec((2 * SEQ, width), lambda s: (s, 0))


def whole(rows, width):
    return pl.BlockSpec((rows, width), lambda s: (0, 0))


SMALL = pl.CostEstimate(flops=2**20, bytes_accessed=2**16, transcendentals=0)
KERNEL_SPACE = pltpu.CompilerParams(vmem_limit_bytes=16 * 2**20)


AS_IT_LIES = pl.BlockSpec(memory_space=pl.ANY)
HEADS_SCRATCH = [
    pltpu.VMEM((2, 2, 2, 2, D // 16, 6 * HD), LOW),
    pltpu.SemaphoreType.DMA((2,)),
]


def heads_forward(link, inputs, weight, cosine, sine, gain_rows, total):
    tokens = inputs.shape[0]
    return pl.pallas_call(
        functools.partial(heads_kernel, link),
        grid=(tokens // (2 * SEQ),),
        in_specs=[
            by_sequence(D),
            AS_IT_LIES,
            AS_IT_LIES,
            by_sequence(HD),
            by_sequence(HD),
            whole(8, HD),
            by_sequence(D),
        ],
        out_specs=[by_sequence(4 * HD), by_sequence(2 * HD), by_sequence(D)],
        out_shape=[
            jax.ShapeDtypeStruct((tokens, 4 * HD), F32),
            jax.ShapeDtypeStruct((tokens, 2 * HD), LOW),
            jax.ShapeDtypeStruct((tokens, D), F32),
        ],
        scratch_shapes=HEADS_SCRATCH,
        compiler_params=KERNEL_SPACE,
        cost_estimate=SMALL,
    )(inputs, *weight, cosine, sine, gain_rows, total)


def heads_backward(link, raw, branch, weight, cosine, sine, gain_rows, total):
    tokens = raw.shape[0]
    grad_raw, terms, total = pl.pallas_call(
        functools.partial(heads_back_kernel, link),
        grid=(tokens // (2 * SEQ),),
        in_specs=[
            by_sequence(4 * HD),
            by_sequence(D),
            AS_IT_LIES,
            AS_IT_LIES,
            by_sequence(HD),
            by_sequence(HD),
            whole(8, HD),
            by_sequence(D),
        ],
        out_specs=[
            by_sequence(4 * HD),
            pl.BlockSpec((8, HD), lambda s: (s, 0)),
            by_sequence(D),
        ],
        out_shape=[
            jax.ShapeDtypeStruct((tokens, 4 * HD), LOW),
            jax.ShapeDtypeStruct((tokens // (2 * SEQ) * 8, HD), F32),
            jax.ShapeDtypeStruct((tokens, D), F32),
        ],
        scratch_shapes=[pltpu.VMEM((2 * SEQ, 2 * HD), LOW), *HEADS_SCRATCH],
        compiler_params=KERNEL_SPACE,
        cost_estimate=SMALL,
    )(raw, branch, *weight, cosine, sine, gain_rows, total)
    return grad_raw, jnp.sum(terms.reshape(-1, 8, HD), axis=0), total


def inner_kernel(input_ref, grad_ref, *refs):
    pieces, (act_ref, inner_ref), sums = refs[:8], refs[8:10], refs[10:14]
    quarters, arrived = refs[14:18], refs[18]
    copies = [
        fetch(pieces[2 * i : 2 * i + 2], quarters[i], arrived.at[i], (3 + i) % 4) for i in range(4)
    ]
    for pair in copies:
        for copy in pair:
            copy.start()
    width = FF // 8
    outward, back = 0.0, 0.0
    for i in range(4):
        for copy in copies[i]:
            copy.wait()
        w = quarters[i].reshape(D, INNER_WIDTH)
        gate_up = dot(input_ref[...], w[:, : 2 * width])
        gate, up = gate_up[:, :width], gate_up[:, width:]
        sigmoid = jax.nn.sigmoid(gate)
        swish = gate * sigmoid
        act = (swish * up).astype(LOW)
        act_ref[:, i * width : (i + 1) * width] = act
        grad_act = dot(grad_ref[...], w[:, 2 * width :])
        slope = sigmoid * (1.0 + gate * (1.0 - sigmoid))
        start = i * 2 * width
        inner_ref[:, start : start + width] = (grad_act * up * slope).astype(LOW)
        inner_ref[:, start + width : start + 2 * width] = (grad_act * swish).astype(LOW)
        outward = outward + dot(act, w[:, 2 * width :], LAST)
        back = back + dot(inner_ref[:, start : start + 2 * width], w[:, : 2 * width], LAST)
    own = outward.shape[0] // 2
    for total, own_ref, other_ref in ((outward, *sums[:2]), (back, *sums[2:])):
        own_ref[...] = total[:own]
        other_ref[...] = total[own:].astype(LOW)


def inner_units(inputs, grads, pieces):
    tokens = inputs.shape[0]
    in_vmem = pl.BlockSpec(memory_space=pltpu.VMEM)
    halves = [
        jax.ShapeDtypeStruct((tokens // 2, D), F32),
        jax.ShapeDtypeStruct((tokens // 2, D), LOW),
    ]
    return pl.pallas_call(
        inner_kernel,
        in_specs=[in_vmem] * 2 + [AS_IT_LIES] * 8,
        out_specs=[in_vmem] * 6,
        out_shape=[
            jax.ShapeDtypeStruct((tokens, FF // 2), LOW),
            jax.ShapeDtypeStruct((tokens, FF), LOW),
            *halves,
            *halves,
        ],
        scratch_shapes=[
            *[pltpu.VMEM((2, 2, 2, 2, D // 16, INNER_WIDTH), LOW)] * 4,
            pltpu.SemaphoreType.DMA((4, 2)),
        ],
        compiler_params=pltpu.CompilerParams(vmem_limit_bytes=36 * 2**20),
        cost_estimate=SMALL,
    )(inputs, grads, *pieces)


def terms_kernel(link, first_left, first_right, second_left, second_right, kept_ref, sent_ref):
    width = first_right.shape[1]
    first = dot(first_left[...], first_right[...], ROWS).astype(LOW)
    second = dot(second_left[...], second_right[...], ROWS).astype(LOW)

    def put(ref, to, start, rows):
        ref[to : to + rows, :width] = first[start : start + rows]
        ref[to : to + rows, width:] = second[start : start + rows]

    if link < 2:
        block = pl.program_id(0)
        part = block // 2 if link == 0 else block % 2

        @pl.when(part == 0)
        def _():
            put(kept_ref, 0, 0, BLOCK)

        @pl.when(part == 1)
        def _():
            put(sent_ref, 0, 0, BLOCK)

    else:
        rows = 128 if link == 2 else 64
        for start in range(0, BLOCK, 2 * rows):
            put(kept_ref, start // 2, start, rows)
            put(sent_ref, start // 2, start + rows, rows)


def terms(link, first_left, first_right, second_left, second_right):
    tokens = first_left.shape[0]

    def right(x, at, width):
        return x, pl.BlockSpec((tokens, width), lambda r: (0, at))

    left = pl.BlockSpec((tokens, BLOCK), lambda r: (0, r))
    operands = [(first_left, left), right(*first_right), (second_left, left), right(*second_right)]
    width = first_right[2] + second_right[2]
    if link == 0:
        specs = [
            pl.BlockSpec((BLOCK, width), lambda r: (jnp.minimum(r, 1), 0)),
            pl.BlockSpec((BLOCK, width), lambda r: (jnp.maximum(r - 2, 0), 0)),
        ]
    elif link == 1:
        specs = [pl.BlockSpec((BLOCK, width), lambda r: (r // 2, 0))] * 2
    else:
        specs = [pl.BlockSpec((BLOCK // 2, width), lambda r: (r, 0))] * 2
    half = jax.ShapeDtypeStruct((D // 2, width), LOW)
    kept, sent = pl.pallas_call(
        functools.partial(terms_kernel, link),
        grid=(4,),
        in_specs=[spec for _, spec in operands],
        out_specs=specs,
        out_shape=[half, half],
        compiler_params=KERNEL_SPACE,
        cost_estimate=SMALL,
    )(*[x for x, _ in operands])
    shape = [2, 2, 2, 2, D // 16, width]
    shape[link] = 1
    return kept.reshape(shape), sent.reshape(shape)


def shared_sum(partial):
    own = partial.shape[0] // 2
    return partial[:own] + swap(partial[own:].astype(LOW)).astype(F32)


def both(x):
    return jnp.concatenate([x, swap(x)], axis=0)


def norm_back(grad_hat, normed, scale):
    return scale * (grad_hat - normed * jnp.mean(grad_hat * normed, axis=-1, keepdims=True))


HEADS_WIDTH, INNER_WIDTH = 6 * HD, 3 * FF // 8


def pieces_of(core):
    pieces = []
    for i in range(core * 4, core * 4 + 4):
        pieces += [(0, i * 2 * HD, 2 * HD), (1, i * HD, HD), (2, i * HD, HD), (3, i * 2 * HD, 2 * HD)]
    for i in range(core * 4, core * 4 + 4):
        pieces += [(m, i * FF // 8, FF // 8) for m in (4, 5, 6)]
    return pieces


HALF_WIDTH = sum(WIDTHS) // 2


def compact_kernel(at_ref, top_ref, low_ref, mine_ref, theirs_ref):
    for core in range(2):

        @pl.when(at_ref[7] == core)
        def _():
            for out_ref, pieces in ((mine_ref, pieces_of(core)), (theirs_ref, pieces_of(1 - core))):
                to = 0
                for m, start, width in pieces:
                    out_ref[:16, to : to + width] = top_ref[at_ref[m], :, start : start + width]
                    out_ref[16:, to : to + width] = low_ref[at_ref[m], :, start : start + width]
                    to += width


def compact(at, top, low):
    half = jax.ShapeDtypeStruct((32, HALF_WIDTH), LOW)
    in_vmem = pl.BlockSpec(memory_space=pltpu.VMEM)
    return pl.pallas_call(
        compact_kernel,
        in_specs=[pl.BlockSpec(memory_space=pltpu.SMEM), in_vmem, in_vmem],
        out_specs=[in_vmem, in_vmem],
        out_shape=[half, half],
        compiler_params=pltpu.CompilerParams(vmem_limit_bytes=24 * 2**20),
        cost_estimate=pl.CostEstimate(flops=0, bytes_accessed=5 * 2**20, transcendentals=0),
    )(at, top, low)


def route_kernel(of_ref, kept_ref, got_ref, top_keep, top_send, low_keep, low_send, held):
    held[...] = jnp.zeros_like(held)
    for core in range(2):

        @pl.when(of_ref[8] == core)
        def _():
            for in_ref, pieces in ((kept_ref, pieces_of(core)), (got_ref, pieces_of(1 - core))):
                at = 0
                for m, start, width in pieces:
                    held[m, :, start : start + width] = in_ref[:, at : at + width]
                    at += width

    for place in range(8):
        near, far, j = place // 4, (place // 2) % 2, place % 2
        (top_keep, top_send)[near][2 * far + j] = held[of_ref[place], :16, :]
        (low_keep, low_send)[far][2 * near + j] = held[of_ref[place], 16:, :]


def route(of, kept, got):
    half = jax.ShapeDtypeStruct((4, 16, FF), LOW)
    in_vmem = pl.BlockSpec(memory_space=pltpu.VMEM)
    return pl.pallas_call(
        route_kernel,
        in_specs=[pl.BlockSpec(memory_space=pltpu.SMEM), in_vmem, in_vmem],
        out_specs=[in_vmem] * 4,
        out_shape=[half] * 4,
        scratch_shapes=[pltpu.VMEM((8, 32, FF), LOW)],
        compiler_params=pltpu.CompilerParams(vmem_limit_bytes=24 * 2**20),
        cost_estimate=pl.CostEstimate(flops=0, bytes_accessed=5 * 2**20, transcendentals=0),
    )(of, kept, got)


def shards(
    hidden_in,
    out_grad,
    seq_owner,
    token_place,
    matrix_slot,
    weight_slots,
    momentum_slots,
    gains,
    gain_momentum,
):
    slot_count, length = hidden_in.shape[:2]
    tok_count = slot_count * length
    z, y = lax.axis_index("dp_0"), lax.axis_index("dp_1")
    core, group = lax.axis_index("dp_2"), lax.axis_index("group")
    first_core = core == 0
    replica = ((z * 4 + y) * 2 + core) * 4 + group

    def core_pick(zero, one):
        return jnp.where(first_core, zero, one)

    weight_low = weight_slots.astype(LOW)
    (slots_top, slots_low), hidden_in = gather_group(
        [weight_low[:, :16], weight_low[:, 16:]], hidden_in
    )
    at = place_of(jnp.bitwise_xor(group, matrix_slot >> 1)) * 2 + (matrix_slot & 1)
    mine, theirs = compact(jnp.concatenate([at, core[None]]), slots_top, slots_low)
    got = swap(theirs)
    chip_rows = core_pick(
        jnp.concatenate([mine, got], axis=0), jnp.concatenate([got, mine], axis=0)
    )
    heads_held = gather_shaped(chip_rows[:, : 4 * HEADS_WIDTH], HEADS_WIDTH)
    inner_held = gather_shaped(chip_rows[:, 4 * HEADS_WIDTH :], INNER_WIDTH)
    column = lax.broadcasted_iota(jnp.int32, (D, D), 1)
    source = lax.broadcasted_iota(jnp.int32, (D, D), 0)
    block = column // 64
    near_z, near_y = block // 8, (block // 4) % 2
    far_z, far_y = (block // 2) % 2, block % 2
    from_z = jnp.bitwise_xor(z, jnp.bitwise_xor(near_z, far_z * 3))
    from_y = jnp.bitwise_xor(y, jnp.bitwise_xor(near_y, far_y * 3))
    reorder = (source == (from_z * 4 + from_y) * 64 + column % 64).astype(LOW)

    live_count = jnp.sum((seq_owner == replica).astype(jnp.int32))
    live_slot = (jnp.arange(slot_count, dtype=jnp.int32) < live_count).astype(F32)
    live_token = jnp.repeat(live_slot, length)[:, None]
    tokens = dot(hidden_in.reshape(tok_count, D), reorder)
    grad_out = dot(out_grad.reshape(tok_count, D), reorder) * live_token
    grad_low = both(grad_out.astype(LOW))
    layer_gains = jnp.dot(
        gains[: 2 * D].reshape(2, D), reorder.astype(F32), precision=lax.Precision.HIGHEST
    )
    gain_one, gain_two = layer_gains[0:1], layer_gains[1:2]
    gain_rows = jnp.pad(gains[2 * D :].reshape(2, HD), ((0, 6), (0, 0)))
    places = both(token_place).astype(F32).reshape(-1, 1)
    exponent = jnp.arange(HD // 2, dtype=F32) * (-2.0 / HD)
    angles = places * jnp.power(rope_base, exponent)[None, :]
    cosine, sine = jnp.cos(angles), jnp.sin(angles)
    cosine = jnp.concatenate([cosine, cosine], axis=1)
    sine = jnp.concatenate([-sine, sine], axis=1)

    scale_one = lax.rsqrt(jnp.mean(tokens * tokens, axis=-1, keepdims=True) + norm_eps)
    normed_one = tokens * scale_one
    input_one = both((normed_one * gain_one).astype(LOW))
    heads_held = together(gather_step(heads_held, 0))
    held = together([*gather_step(heads_held, 1), *gather_step(inner_held, 0)])
    held = together([*gather_step(held[:4], 2), *gather_step(held[4:], 1)])
    heads_held, inner_held = held[:4], held[4:]
    held = together([*gather_came(heads_held, 3), *gather_step(inner_held, 2)])
    w_heads = list(zip(heads_held, held[:4]))
    inner_held = held[4:]
    w_inner = [x for pair in zip(inner_held, gather_came(inner_held, 3)) for x in pair]
    raw, attn = [], []
    branch = jnp.zeros((2 * tok_count, D), F32)
    for i in range(4):
        fresh, heads, branch = heads_forward(
            (3 + i) % 4, input_one, w_heads[i], cosine, sine, gain_rows, branch
        )
        raw.append(fresh)
        attn.append(heads)
    *w_inner, branch = together([*w_inner, branch])
    residual = tokens + shared_sum(branch)
    scale_two = lax.rsqrt(jnp.mean(residual * residual, axis=-1, keepdims=True) + norm_eps)
    normed_two = residual * scale_two
    input_two = both((normed_two * gain_two).astype(LOW))
    act, grad_inner, outward, outward_other, grad_two, grad_two_other = inner_units(
        input_two, grad_low, w_inner
    )
    result = (residual + (outward + swap(outward_other).astype(F32))) * live_token
    hidden_out = dot(result.astype(LOW), reorder, LAST).astype(LOW)

    sent, kept = [], []
    for i in range(4):
        keep, send = terms(
            i, input_two, (grad_inner, i, FF // 4), grad_low, (act, i, FF // 8)
        )
        sent.append(send)
        kept.append(keep)
    grad_two = grad_two + swap(grad_two_other).astype(F32)
    gain_two_term = jnp.sum(grad_two * normed_two, axis=0, keepdims=True)
    grad_residual = grad_out + norm_back(grad_two * gain_two, normed_two, scale_two)
    branch_low = both(grad_residual.astype(LOW))
    grad_one, head_terms, grad_raw = jnp.zeros((2 * tok_count, D), F32), 0.0, []
    heads_sent, heads_kept = [], []

    def back_through(i, branch, grad_one):
        fresh, term, grad_one = heads_backward(
            (3 + i) % 4, raw[i], branch, w_heads[i], cosine, sine, gain_rows, grad_one
        )
        grad_raw.append(fresh)
        return head_terms + term, grad_one

    def heads_terms(i):
        keep, send = terms(
            i, input_one, (grad_raw[i], 0, 4 * HD), branch_low, (attn[i], 0, 2 * HD)
        )
        heads_kept.append(keep)
        heads_sent.append(send)

    head_terms, grad_one = back_through(0, branch_low, grad_one)
    head_terms, grad_one = back_through(1, branch_low, grad_one)
    sent, kept = scatter_step(sent, kept, 0)
    *held, branch_low, grad_one = together([*sent, *kept, branch_low, grad_one])
    sent, kept = held[:4], held[4:]
    head_terms, grad_one = back_through(2, branch_low, grad_one)
    heads_terms(0)
    sent, kept = scatter_step(sent, kept, 1)
    *held, branch_low, heads_sent[0], grad_one = together(
        [*sent, *kept, branch_low, heads_sent[0], grad_one]
    )
    sent, kept = held[:4], held[4:]
    head_terms, grad_one = back_through(3, branch_low, grad_one)
    heads_terms(1)
    sent, kept = scatter_step(sent, kept, 2)
    *held, heads_sent[1], grad_one = together([*sent, *kept, heads_sent[1], grad_one])
    sent, kept = held[:4], held[4:]
    heads_terms(2)
    heads_terms(3)
    sent, kept = scatter_step(sent, kept, 3)
    inner_sums = flat(kept)
    sent, kept = heads_sent, heads_kept
    grad_one = shared_sum(grad_one)
    gain_one_term = jnp.sum(grad_one * normed_one, axis=0, keepdims=True)
    in_grad = grad_residual + norm_back(grad_one * gain_one, normed_one, scale_one)
    in_high, in_low = split_two(in_grad)
    in_grad = dot(in_high, reorder, LAST) + dot(in_low, reorder, LAST)
    layer_terms = lax.dot_general(
        jnp.concatenate([gain_one_term, gain_two_term], axis=0),
        reorder.astype(F32),
        (LAST, ((), ())),
        precision=lax.Precision.HIGHEST,
    )
    gain_sum = jnp.concatenate([layer_terms.reshape(-1), head_terms[:2].reshape(-1)])
    for step in range(4):
        sent, kept = scatter_step(sent, kept, step)
        if step == 1:
            gain_sum = gain_sum + swap(gain_sum)
        elif step > 1:
            gain_sum = gain_sum + lax.ppermute(gain_sum, "group", (NEAR, FAR)[step - 2])
        if step == 0:
            *held, in_grad, gain_sum = together([*sent, *kept, in_grad, gain_sum])
        else:
            *held, gain_sum = together([*sent, *kept, gain_sum])
        sent, kept = held[:-4], held[-4:]
    heads_sums = flat(kept)

    sums = jnp.concatenate([*heads_sums, *inner_sums], axis=1)
    kept = core_pick(sums[:32], sums[32:])
    got = swap(core_pick(sums[32:], sums[:32]))
    slot_at = (jnp.bitwise_xor(group, jnp.asarray(MASKS, jnp.int32)) * 2)[:, None]
    slot_at = (slot_at + jnp.arange(2, dtype=jnp.int32)[None, :]).reshape(8)
    matches = slot_at[:, None] == matrix_slot[None, :]
    numbers = jnp.arange(7, dtype=jnp.int32)[None, :]
    routed_from = 7 - jnp.max(jnp.where(matches, 7 - numbers, 0), axis=1)
    halves = route(jnp.concatenate([routed_from, core[None]]), kept, got)
    sent, kept = [halves[1], halves[3]], [halves[0], halves[2]]
    for step in range(2):
        got = together(
            [lax.ppermute(sent[i], "group", (NEAR, FAR)[(step + i) % 2]) for i in range(2)]
        )
        total = [kept[i].astype(F32) + got[i].astype(F32) for i in range(2)]
        if step == 0:
            held = together([*(t[2:].astype(LOW) for t in total), *(t[:2].astype(LOW) for t in total)])
            sent, kept = held[:2], held[2:]
    weight_grad = jnp.concatenate(total, axis=1)

    own_ids = group * 2 + jnp.arange(2, dtype=jnp.int32)
    own_match = own_ids[:, None] == matrix_slot[None, :]
    own_width = jnp.sum(jnp.where(own_match, jnp.asarray(WIDTHS, jnp.int32)[None, :], 0), axis=1)
    own_width = own_width.astype(jnp.int32)
    column_mask = (jnp.arange(FF, dtype=jnp.int32)[None, :] < own_width[:, None]).astype(F32)
    column_mask = column_mask[:, None, :]
    momentum_new = column_mask * (momentum_keep * momentum_slots + weight_grad)
    direction = (weight_grad + momentum_keep * momentum_new).astype(LOW)

    mine = core_pick(direction[0], direction[1])
    got = swap(core_pick(direction[1], direction[0]))
    rows = core_pick(jnp.concatenate([mine, got], axis=0), jnp.concatenate([got, mine], axis=0))
    gain_parts, rest = [], gain_sum
    for _ in range(3):
        part = lax.reduce_precision(rest, exponent_bits=8, mantissa_bits=7)
        gain_parts.append(part.astype(LOW))
        rest = rest - part
    gain_parts = jnp.pad(jnp.concatenate(gain_parts), (0, 64 * HD - 3 * gain_sum.shape[0]))
    held = gather_shaped(rows, FF // 4)
    held[0] = jnp.concatenate([held[0], gain_parts.reshape(1, 1, 1, 1, 64, HD)], axis=-1)
    for step in range(3):
        held = together(gather_step(held, step))
    fresh = gather_came(held, 3)
    pieces = [x for pair in zip(held, fresh) for x in pair]
    gain_parts = jnp.concatenate([x[..., FF // 4 :] for x in pieces[:2]], axis=3)
    gain_parts = gain_parts.reshape(16, 64 * HD)
    place = lax.broadcasted_iota(jnp.int32, (16, 16), 1)
    of_z = jnp.bitwise_xor(z, jnp.bitwise_xor(place // 8, (place // 2) % 2 * 3))
    of_y = jnp.bitwise_xor(y, jnp.bitwise_xor((place // 4) % 2, place % 2 * 3))
    in_turn = (lax.broadcasted_iota(jnp.int32, (16, 16), 0) == of_z * 4 + of_y).astype(LOW)
    gain_parts = dot(in_turn, gain_parts)[:, : 3 * gain_sum.shape[0]].reshape(16, 3, -1)
    gain_grad = jnp.sum(gain_parts[:, 0] + gain_parts[:, 1] + gain_parts[:, 2], axis=0)
    iterate = iterate_rows(pieces)
    kept = core_pick(iterate[:32], iterate[32:])
    got = swap(core_pick(iterate[32:], iterate[:32]))
    iterate = jnp.stack([core_pick(kept, got), core_pick(got, kept)]).astype(F32)
    update_scale = 0.2 * jnp.sqrt(jnp.maximum(own_width, D).astype(F32))
    weight_new = column_mask * (
        weight_slots * (1.0 - learn_rate * weight_decay)
        - learn_rate * update_scale[:, None, None] * iterate
    )

    gain_momentum_new = momentum_keep * gain_momentum + gain_grad
    gain_step = gain_grad + momentum_keep * gain_momentum_new
    rows = gain_step.reshape(18, HD)
    part = jnp.minimum(jnp.arange(18) // 8, 1) + (jnp.arange(18) // 16) * (jnp.arange(18) - 15)
    alike = part[:, None] == part[None, :]
    squares = jnp.sum(rows * rows, axis=1)
    sums = jnp.sum(jnp.where(alike, squares[None, :], 0.0), axis=1, keepdims=True)
    counts = jnp.sum(jnp.where(alike, float(HD), 0.0), axis=1, keepdims=True)
    scaled = rows * lax.rsqrt(sums / counts + norm_eps)
    gain_new = gains - gain_rate * scaled.reshape(-1)
    shape = (slot_count, length, D)
    return (
        hidden_out.reshape(shape),
        in_grad.reshape(shape),
        weight_grad,
        momentum_new,
        weight_new,
        gain_grad,
        gain_momentum_new,
        gain_new,
    )


def solution(mesh):
    finer = Mesh(
        mesh.devices.reshape(4, 4, 2, mesh.shape["group"]), ("dp_0", "dp_1", "dp_2", "group")
    )
    in_specs = (
        P(DP_GROUP, None, None),
        P(DP_GROUP, None, None),
        P(),
        P(DP_GROUP, None),
        P(),
        P("group", ("dp_0", "dp_1", "dp_2"), None),
        P("group", ("dp_0", "dp_1", "dp_2"), None),
        P(),
        P(),
    )
    out_specs = (
        P(DP_GROUP, None, None),
        P(DP_GROUP, None, None),
        P("group", ("dp_0", "dp_1", "dp_2"), None),
        P("group", ("dp_0", "dp_1", "dp_2"), None),
        P("group", ("dp_0", "dp_1", "dp_2"), None),
        P(),
        P(),
        P(),
    )
    return jax.shard_map(
        shards, mesh=finer, in_specs=in_specs, out_specs=out_specs, check_vma=False
    )
```

```python
import functools

import jax
import jax.numpy as jnp
from jax import lax
from jax.experimental import pallas as pl
from jax.experimental.pallas import tpu as pltpu
from jax.sharding import Mesh
from jax.sharding import PartitionSpec as P

D = 1024
HEADS = 16
KV = 8
HD = 128
FF = 3072
SEQ = 128
NS_ITERS = 5
WIDTHS = (HEADS * HD, KV * HD, KV * HD, HEADS * HD, FF, FF, FF)
DP_GROUP = ("dp_0", "dp_1", "dp_2", "group")
LOW = jnp.bfloat16
F32 = jnp.float32

norm_eps = 1e-06
frob_eps = 1e-07
rope_base = 1000000.0
coef_linear = 3.4445
coef_square = -4.775
coef_quartic = 2.0315
momentum_keep = 0.95
learn_rate = 0.15
weight_decay = 0.1
gain_rate = 0.5
masked_score = -1e30
score_scale = HD ** (-0.5)

NEAR = ((0, 1), (1, 0), (2, 3), (3, 2))
FAR = ((0, 3), (3, 0), (1, 2), (2, 1))
LINKS = (("dp_0", NEAR), ("dp_1", NEAR), ("dp_0", FAR), ("dp_1", FAR))
MASKS = (0, 3, 1, 2)


def place_of(mask):
    return jnp.where(mask == 0, 0, jnp.where(mask == 3, 1, mask + 1))


def swap(x):
    return lax.ppermute(x, "dp_2", ((0, 1), (1, 0)))


def together(arrays):
    return list(lax.optimization_barrier(tuple(arrays)))


def gather_came(quarters, step):
    fresh = []
    for i in range(4):
        axis, pairs = LINKS[(step + i) % 4]
        fresh.append(lax.ppermute(quarters[i], axis, pairs))
    return together(fresh)


def gather_step(quarters, step):
    fresh = gather_came(quarters, step)
    return [
        jnp.concatenate([quarters[i], fresh[i]], axis=(step + i) % 4) for i in range(4)
    ]


def gather_shaped(x, width):
    return [
        x[:, i * width : (i + 1) * width].reshape(1, 1, 1, 1, x.shape[0], width) for i in range(4)
    ]


def flat(quarters):
    return [q.reshape(-1, q.shape[-1]) for q in quarters]


def scatter_step(sent, kept, step):
    to_send, to_keep, came = [], [], []
    for i in range(4):
        axis, pairs = LINKS[(step + i) % 4]
        came.append(lax.ppermute(sent[i], axis, pairs))
    came = together(came)
    for i in range(4):
        at = (step + 1 + i) % 4

        def half(part):
            if step == 3:
                return (kept[i].astype(F32) + came[i].astype(F32)).astype(LOW)
            both_parts = [lax.slice_in_dim(x, part, part + 1, axis=at) for x in (kept[i], came[i])]
            return (both_parts[0].astype(F32) + both_parts[1].astype(F32)).astype(LOW)

        to_keep.append(half(0))
        if step < 3:
            to_send.append(half(1))
    return to_send, to_keep


def gather_group(halves, after):
    held = [h[None, None] for h in halves]
    for step in range(2):
        fresh = [lax.ppermute(held[i], "group", (NEAR, FAR)[(step + i) % 2]) for i in range(2)]
        if step == 0:
            *fresh, after = together([*fresh, after])
        held = [jnp.concatenate([held[i], fresh[i]], axis=(step + i) % 2) for i in range(2)]
    return [h.reshape(8, *h.shape[3:]) for h in held], after


def dot(left, right, dims=((1,), (0,))):
    return lax.dot_general(left, right, (dims, ((), ())), preferred_element_type=F32)


ROWS = ((0,), (0,))
LAST = ((1,), (1,))
PLAIN = ((1,), (0,))


def split_two(x):
    high = lax.reduce_precision(x, exponent_bits=8, mantissa_bits=7)
    return high.astype(LOW), (x - high).astype(LOW)


def half_turn(u):
    return jnp.concatenate([u[:, HD // 2 :], u[:, : HD // 2]], axis=1)


def fetch(pieces, quarter, arrived, link):
    copies = []
    for part in range(2):
        place = [slice(None)] * 4
        place[link] = slice(part, part + 1)
        copies.append(
            pltpu.make_async_copy(pieces[part], quarter.at[tuple(place)], arrived.at[part])
        )
    return copies


def head_forward(raw, gain, cosine, sine):
    scale = lax.rsqrt(jnp.mean(raw * raw, axis=-1, keepdims=True) + norm_eps)
    normed = raw * scale
    gained = normed * gain
    turned = gained * cosine + half_turn(gained) * sine
    return normed, scale, turned.astype(LOW)


def softmax_parts(query, key):
    scores = dot(query, key, LAST) * score_scale
    rows = lax.broadcasted_iota(jnp.int32, scores.shape, 0) & (SEQ - 1)
    columns = lax.broadcasted_iota(jnp.int32, scores.shape, 1)
    scores = jnp.where(rows >= columns, scores, masked_score)
    terms = jnp.exp(scores - jnp.max(scores, axis=-1, keepdims=True))
    return terms / jnp.sum(terms, axis=-1, keepdims=True)


def two_heads(ref, at):
    return jnp.concatenate([ref[at, :HD], ref[at, HD : 2 * HD]], axis=0)


def twice(x):
    return jnp.concatenate([x, x], axis=0)


def heads_kernel(
    link,
    input_ref,
    held_ref,
    fresh_ref,
    cos_ref,
    sin_ref,
    gain_ref,
    sum_ref,
    raw_ref,
    attn_ref,
    out_ref,
    quarter,
    arrived,
):
    @pl.when(pl.program_id(0) == 0)
    def _():
        copies = fetch((held_ref, fresh_ref), quarter, arrived, link)
        for copy in copies:
            copy.start()
        for copy in copies:
            copy.wait()

    weight_ref = quarter.reshape(D, HEADS_WIDTH)
    raw_ref[...] = dot(input_ref[...], weight_ref[:, : 4 * HD])
    for b in range(raw_ref.shape[0] // SEQ):
        at = slice(b * SEQ, (b + 1) * SEQ)
        cosine, sine = cos_ref[at, :], sin_ref[at, :]
        _, _, key = head_forward(raw_ref[at, 2 * HD : 3 * HD], gain_ref[1:2, :], cosine, sine)
        value = raw_ref[at, 3 * HD :].astype(LOW)
        _, _, query = head_forward(
            two_heads(raw_ref, at), gain_ref[0:1, :], twice(cosine), twice(sine)
        )
        probs = softmax_parts(query, key).astype(LOW)
        out = dot(probs, value).astype(LOW)
        attn_ref[at, :HD] = out[:SEQ]
        attn_ref[at, HD:] = out[SEQ:]
    out_ref[...] = sum_ref[...] + dot(attn_ref[...], weight_ref[:, 4 * HD :], LAST)


def head_backward(grad, normed, scale, gain, cosine, sine):
    back = grad * cosine - half_turn(grad) * sine
    term = jnp.sum(back * normed, axis=0, keepdims=True)
    g = back * gain
    raw = scale * (g - normed * jnp.mean(g * normed, axis=-1, keepdims=True))
    return raw.astype(LOW), term


def heads_back_kernel(
    link,
    raw_ref,
    branch_ref,
    held_ref,
    fresh_ref,
    cos_ref,
    sin_ref,
    gain_ref,
    sum_ref,
    out_ref,
    term_ref,
    one_ref,
    grad_ref,
    quarter,
    arrived,
):
    @pl.when(pl.program_id(0) == 0)
    def _():
        copies = fetch((held_ref, fresh_ref), quarter, arrived, link)
        for copy in copies:
            copy.start()
        for copy in copies:
            copy.wait()

    weight_ref = quarter.reshape(D, HEADS_WIDTH)
    grad_ref[...] = dot(branch_ref[...], weight_ref[:, 4 * HD :]).astype(LOW)
    query_terms, key_terms = 0.0, 0.0
    for b in range(raw_ref.shape[0] // SEQ):
        at = slice(b * SEQ, (b + 1) * SEQ)
        cosine, sine = cos_ref[at, :], sin_ref[at, :]
        cosines, sines = twice(cosine), twice(sine)
        key_hat, key_scale, key = head_forward(
            raw_ref[at, 2 * HD : 3 * HD], gain_ref[1:2, :], cosine, sine
        )
        value = raw_ref[at, 3 * HD :].astype(LOW)
        query_hat, query_scale, query = head_forward(
            two_heads(raw_ref, at), gain_ref[0:1, :], cosines, sines
        )
        probs = softmax_parts(query, key)
        grad_attn = two_heads(grad_ref, at)
        grad_value = dot(probs.astype(LOW), grad_attn, ROWS)
        grad_probs = dot(grad_attn, value, LAST)
        inner = jnp.sum(probs * grad_probs, axis=-1, keepdims=True)
        grad_scores = (probs * (grad_probs - inner)).astype(LOW)
        grad_query = dot(grad_scores, key) * score_scale
        grad_key = dot(grad_scores, query, ROWS) * score_scale
        raw, term = head_backward(
            grad_query, query_hat, query_scale, gain_ref[0:1, :], cosines, sines
        )
        query_terms = query_terms + term
        out_ref[at, :HD] = raw[:SEQ]
        out_ref[at, HD : 2 * HD] = raw[SEQ:]
        raw, term = head_backward(grad_key, key_hat, key_scale, gain_ref[1:2, :], cosine, sine)
        key_terms = key_terms + term
        out_ref[at, 2 * HD : 3 * HD] = raw
        out_ref[at, 3 * HD :] = grad_value.astype(LOW)
    spare = jnp.zeros((6, HD), F32)
    term_ref[...] = jnp.concatenate([query_terms, key_terms, spare], axis=0)
    one_ref[...] = sum_ref[...] + dot(out_ref[...], weight_ref[:, : 4 * HD], LAST)


BLOCK = D // 4


def iterate_kernel(*refs):
    pieces, out_ref, refs = refs[:8], refs[8], refs[9:]
    quarters, gram, high, low, poly, mixed_high, mixed_low, own, arrived = refs[:4], *refs[4:]
    copies = [
        copy
        for i in range(4)
        for copy in fetch(pieces[2 * i : 2 * i + 2], quarters[i], arrived.at[i], (3 + i) % 4)
    ]
    for copy in copies:
        copy.start()
    for copy in copies:
        copy.wait()
    x0, x1, x2, x3 = [q.reshape(D, q.shape[-1]) for q in quarters]
    at = [slice(i * BLOCK, (i + 1) * BLOCK) for i in range(4)]
    blocks = [(i, j) for i in range(4) for j in range(4)]

    def parts(x):
        top = x.astype(LOW)
        return top, (x - top.astype(F32)).astype(LOW)

    def mirrored(ref, i, j, block):
        ref[at[i], at[j]] = block.astype(ref.dtype)
        if i != j:
            ref[at[j], at[i]] = block.T.astype(ref.dtype)

    def two_dot(left, right):
        rows = left.shape[0]
        both_parts = dot(jnp.concatenate(parts(left), axis=0), right)
        return both_parts[:rows] + both_parts[rows:]

    rows = lax.broadcasted_iota(jnp.int32, (BLOCK, BLOCK), 0)
    columns = lax.broadcasted_iota(jnp.int32, (BLOCK, BLOCK), 1)
    trace = jnp.zeros((1, 1), F32)
    for i, j in blocks:
        if j > i:
            continue
        block = sum(
            dot(x[at[i], : FF // 4], x[at[j], : FF // 4], LAST) for x in (x0, x1, x2, x3)
        )
        mirrored(gram, i, j, block)
        if i == j:
            diagonal = jnp.where(rows == columns, block, 0.0)
            trace = trace + jnp.sum(jnp.sum(diagonal, axis=1, keepdims=True), axis=0, keepdims=True)
    inverse = 1.0 / (jnp.sqrt(trace) + frob_eps)
    for i, j in blocks:
        block = gram[at[i], at[j]] * (inverse * inverse)
        gram[at[i], at[j]] = block
        high[at[i], at[j]], low[at[i], at[j]] = parts(block)
    own_rows = lax.broadcasted_iota(jnp.int32, own.shape, 0)
    own[...] = (own_rows == lax.broadcasted_iota(jnp.int32, own.shape, 1)).astype(F32)

    def set_poly():
        for i, j in blocks:
            if j > i:
                continue
            square = dot(high[at[i], :], high[:, at[j]])
            block = coef_square * high[at[i], at[j]].astype(F32) + coef_quartic * square
            mirrored(poly, i, j, block)

    def through_poly(x):
        return coef_linear * x + two_dot(x, poly[...])

    def sweep(_, carry):
        set_poly()
        own[...] = through_poly(own[...])
        for i, j in blocks:
            block = dot(high[at[i], :], poly[:, at[j]]) + dot(low[at[i], :], poly[:, at[j]])
            gram[at[i], at[j]] = (coef_linear * coef_linear) * gram[at[i], at[j]] + (
                2.0 * coef_linear
            ) * block
            mixed_high[at[i], at[j]], mixed_low[at[i], at[j]] = parts(block)
        for i, j in blocks:
            block = dot(mixed_high[at[i], :], poly[:, at[j]])
            block = block + dot(mixed_low[at[i], :], poly[:, at[j]]) + gram[at[i], at[j]]
            gram[at[i], at[j]] = block
            high[at[i], at[j]], low[at[i], at[j]] = parts(block)
        return carry

    lax.fori_loop(0, NS_ITERS - 2, sweep, 0)
    set_poly()
    own[...] = through_poly(own[...])

    def through_next(x):
        x = through_poly(x)
        x = two_dot(x, high[...]) + dot(x.astype(LOW), low[...])
        return through_poly(x)

    once = through_next(own[...])
    second = through_next(once)
    last = coef_linear * own[...] + coef_square * once + coef_quartic * second
    last = last * inverse
    for k, x in enumerate((x0, x1, x2, x3)):
        width = FF // 4
        out_ref[:, k * width : (k + 1) * width] = two_dot(last, x[:, :width]).astype(LOW)


def iterate_rows(pieces):
    square = pltpu.VMEM((D, D), LOW)
    quarters = [pltpu.VMEM((2, 2, 2, 2, D // 16, x.shape[-1]), LOW) for x in pieces[::2]]
    return pl.pallas_call(
        iterate_kernel,
        in_specs=[pl.BlockSpec(memory_space=pl.ANY)] * 8,
        out_specs=pl.BlockSpec(memory_space=pltpu.VMEM),
        out_shape=jax.ShapeDtypeStruct((64, FF), LOW),
        scratch_shapes=[
            *quarters,
            pltpu.VMEM((D, D), F32),
            *[square] * 5,
            pltpu.VMEM((64, D), F32),
            pltpu.SemaphoreType.DMA((4, 2)),
        ],
        compiler_params=pltpu.CompilerParams(vmem_limit_bytes=32 * 2**20),
        cost_estimate=pl.CostEstimate(flops=50 * 10**9, bytes_accessed=2**23, transcendentals=0),
    )(*pieces)


def by_sequence(width):
    return pl.BlockSpec((2 * SEQ, width), lambda s: (s, 0))


def whole(rows, width):
    return pl.BlockSpec((rows, width), lambda s: (0, 0))


SMALL = pl.CostEstimate(flops=2**20, bytes_accessed=2**16, transcendentals=0)
KERNEL_SPACE = pltpu.CompilerParams(vmem_limit_bytes=16 * 2**20)


AS_IT_LIES = pl.BlockSpec(memory_space=pl.ANY)
HEADS_SCRATCH = [
    pltpu.VMEM((2, 2, 2, 2, D // 16, 6 * HD), LOW),
    pltpu.SemaphoreType.DMA((2,)),
]


def heads_forward(link, inputs, weight, cosine, sine, gain_rows, total):
    tokens = inputs.shape[0]
    return pl.pallas_call(
        functools.partial(heads_kernel, link),
        grid=(tokens // (2 * SEQ),),
        in_specs=[
            by_sequence(D),
            AS_IT_LIES,
            AS_IT_LIES,
            by_sequence(HD),
            by_sequence(HD),
            whole(8, HD),
            by_sequence(D),
        ],
        out_specs=[by_sequence(4 * HD), by_sequence(2 * HD), by_sequence(D)],
        out_shape=[
            jax.ShapeDtypeStruct((tokens, 4 * HD), F32),
            jax.ShapeDtypeStruct((tokens, 2 * HD), LOW),
            jax.ShapeDtypeStruct((tokens, D), F32),
        ],
        scratch_shapes=HEADS_SCRATCH,
        compiler_params=KERNEL_SPACE,
        cost_estimate=SMALL,
    )(inputs, *weight, cosine, sine, gain_rows, total)


def heads_backward(link, raw, branch, weight, cosine, sine, gain_rows, total):
    tokens = raw.shape[0]
    grad_raw, terms, total = pl.pallas_call(
        functools.partial(heads_back_kernel, link),
        grid=(tokens // (2 * SEQ),),
        in_specs=[
            by_sequence(4 * HD),
            by_sequence(D),
            AS_IT_LIES,
            AS_IT_LIES,
            by_sequence(HD),
            by_sequence(HD),
            whole(8, HD),
            by_sequence(D),
        ],
        out_specs=[
            by_sequence(4 * HD),
            pl.BlockSpec((8, HD), lambda s: (s, 0)),
            by_sequence(D),
        ],
        out_shape=[
            jax.ShapeDtypeStruct((tokens, 4 * HD), LOW),
            jax.ShapeDtypeStruct((tokens // (2 * SEQ) * 8, HD), F32),
            jax.ShapeDtypeStruct((tokens, D), F32),
        ],
        scratch_shapes=[pltpu.VMEM((2 * SEQ, 2 * HD), LOW), *HEADS_SCRATCH],
        compiler_params=KERNEL_SPACE,
        cost_estimate=SMALL,
    )(raw, branch, *weight, cosine, sine, gain_rows, total)
    return grad_raw, jnp.sum(terms.reshape(-1, 8, HD), axis=0), total


def inner_kernel(input_ref, grad_ref, *refs):
    pieces, (act_ref, inner_ref), sums = refs[:8], refs[8:10], refs[10:14]
    quarters, arrived = refs[14:18], refs[18]
    copies = [
        fetch(pieces[2 * i : 2 * i + 2], quarters[i], arrived.at[i], (3 + i) % 4) for i in range(4)
    ]
    for pair in copies:
        for copy in pair:
            copy.start()
    width = FF // 8
    outward, back = 0.0, 0.0
    for i in range(4):
        for copy in copies[i]:
            copy.wait()
        w = quarters[i].reshape(D, INNER_WIDTH)
        gate_up = dot(input_ref[...], w[:, : 2 * width])
        gate, up = gate_up[:, :width], gate_up[:, width:]
        sigmoid = jax.nn.sigmoid(gate)
        swish = gate * sigmoid
        act = (swish * up).astype(LOW)
        act_ref[:, i * width : (i + 1) * width] = act
        grad_act = dot(grad_ref[...], w[:, 2 * width :])
        slope = sigmoid * (1.0 + gate * (1.0 - sigmoid))
        start = i * 2 * width
        inner_ref[:, start : start + width] = (grad_act * up * slope).astype(LOW)
        inner_ref[:, start + width : start + 2 * width] = (grad_act * swish).astype(LOW)
        outward = outward + dot(act, w[:, 2 * width :], LAST)
        back = back + dot(inner_ref[:, start : start + 2 * width], w[:, : 2 * width], LAST)
    own = outward.shape[0] // 2
    for total, own_ref, other_ref in ((outward, *sums[:2]), (back, *sums[2:])):
        own_ref[...] = total[:own]
        other_ref[...] = total[own:].astype(LOW)


def inner_units(inputs, grads, pieces):
    tokens = inputs.shape[0]
    in_vmem = pl.BlockSpec(memory_space=pltpu.VMEM)
    halves = [
        jax.ShapeDtypeStruct((tokens // 2, D), F32),
        jax.ShapeDtypeStruct((tokens // 2, D), LOW),
    ]
    return pl.pallas_call(
        inner_kernel,
        in_specs=[in_vmem] * 2 + [AS_IT_LIES] * 8,
        out_specs=[in_vmem] * 6,
        out_shape=[
            jax.ShapeDtypeStruct((tokens, FF // 2), LOW),
            jax.ShapeDtypeStruct((tokens, FF), LOW),
            *halves,
            *halves,
        ],
        scratch_shapes=[
            *[pltpu.VMEM((2, 2, 2, 2, D // 16, INNER_WIDTH), LOW)] * 4,
            pltpu.SemaphoreType.DMA((4, 2)),
        ],
        compiler_params=pltpu.CompilerParams(vmem_limit_bytes=36 * 2**20),
        cost_estimate=SMALL,
    )(inputs, grads, *pieces)


def terms_kernel(link, first_left, first_right, second_left, second_right, kept_ref, sent_ref):
    width = first_right.shape[1]
    first = dot(first_left[...], first_right[...], ROWS).astype(LOW)
    second = dot(second_left[...], second_right[...], ROWS).astype(LOW)

    def put(ref, to, start, rows):
        ref[to : to + rows, :width] = first[start : start + rows]
        ref[to : to + rows, width:] = second[start : start + rows]

    if link < 2:
        block = pl.program_id(0)
        part = block // 2 if link == 0 else block % 2

        @pl.when(part == 0)
        def _():
            put(kept_ref, 0, 0, BLOCK)

        @pl.when(part == 1)
        def _():
            put(sent_ref, 0, 0, BLOCK)

    else:
        rows = 128 if link == 2 else 64
        for start in range(0, BLOCK, 2 * rows):
            put(kept_ref, start // 2, start, rows)
            put(sent_ref, start // 2, start + rows, rows)


def terms(link, first_left, first_right, second_left, second_right):
    tokens = first_left.shape[0]

    def right(x, at, width):
        return x, pl.BlockSpec((tokens, width), lambda r: (0, at))

    left = pl.BlockSpec((tokens, BLOCK), lambda r: (0, r))
    operands = [(first_left, left), right(*first_right), (second_left, left), right(*second_right)]
    width = first_right[2] + second_right[2]
    if link == 0:
        specs = [
            pl.BlockSpec((BLOCK, width), lambda r: (jnp.minimum(r, 1), 0)),
            pl.BlockSpec((BLOCK, width), lambda r: (jnp.maximum(r - 2, 0), 0)),
        ]
    elif link == 1:
        specs = [pl.BlockSpec((BLOCK, width), lambda r: (r // 2, 0))] * 2
    else:
        specs = [pl.BlockSpec((BLOCK // 2, width), lambda r: (r, 0))] * 2
    half = jax.ShapeDtypeStruct((D // 2, width), LOW)
    kept, sent = pl.pallas_call(
        functools.partial(terms_kernel, link),
        grid=(4,),
        in_specs=[spec for _, spec in operands],
        out_specs=specs,
        out_shape=[half, half],
        compiler_params=KERNEL_SPACE,
        cost_estimate=SMALL,
    )(*[x for x, _ in operands])
    shape = [2, 2, 2, 2, D // 16, width]
    shape[link] = 1
    return kept.reshape(shape), sent.reshape(shape)


def shared_sum(partial):
    own = partial.shape[0] // 2
    return partial[:own] + swap(partial[own:].astype(LOW)).astype(F32)


def both(x):
    return jnp.concatenate([x, swap(x)], axis=0)


def norm_back(grad_hat, normed, scale):
    return scale * (grad_hat - normed * jnp.mean(grad_hat * normed, axis=-1, keepdims=True))


HEADS_WIDTH, INNER_WIDTH = 6 * HD, 3 * FF // 8


def pieces_of(core):
    pieces = []
    for i in range(core * 4, core * 4 + 4):
        pieces += [(0, i * 2 * HD, 2 * HD), (1, i * HD, HD), (2, i * HD, HD), (3, i * 2 * HD, 2 * HD)]
    for i in range(core * 4, core * 4 + 4):
        pieces += [(m, i * FF // 8, FF // 8) for m in (4, 5, 6)]
    return pieces


HALF_WIDTH = sum(WIDTHS) // 2


def compact_kernel(at_ref, top_ref, low_ref, mine_ref, theirs_ref):
    for core in range(2):

        @pl.when(at_ref[7] == core)
        def _():
            for out_ref, pieces in ((mine_ref, pieces_of(core)), (theirs_ref, pieces_of(1 - core))):
                to = 0
                for m, start, width in pieces:
                    out_ref[:16, to : to + width] = top_ref[at_ref[m], :, start : start + width]
                    out_ref[16:, to : to + width] = low_ref[at_ref[m], :, start : start + width]
                    to += width


def compact(at, top, low):
    half = jax.ShapeDtypeStruct((32, HALF_WIDTH), LOW)
    in_vmem = pl.BlockSpec(memory_space=pltpu.VMEM)
    return pl.pallas_call(
        compact_kernel,
        in_specs=[pl.BlockSpec(memory_space=pltpu.SMEM), in_vmem, in_vmem],
        out_specs=[in_vmem, in_vmem],
        out_shape=[half, half],
        compiler_params=pltpu.CompilerParams(vmem_limit_bytes=24 * 2**20),
        cost_estimate=pl.CostEstimate(flops=0, bytes_accessed=5 * 2**20, transcendentals=0),
    )(at, top, low)


def route_kernel(of_ref, kept_ref, got_ref, top_keep, top_send, low_keep, low_send, held):
    held[...] = jnp.zeros_like(held)
    for core in range(2):

        @pl.when(of_ref[8] == core)
        def _():
            for in_ref, pieces in ((kept_ref, pieces_of(core)), (got_ref, pieces_of(1 - core))):
                at = 0
                for m, start, width in pieces:
                    held[m, :, start : start + width] = in_ref[:, at : at + width]
                    at += width

    for place in range(8):
        near, far, j = place // 4, (place // 2) % 2, place % 2
        (top_keep, top_send)[near][2 * far + j] = held[of_ref[place], :16, :]
        (low_keep, low_send)[far][2 * near + j] = held[of_ref[place], 16:, :]


def route(of, kept, got):
    half = jax.ShapeDtypeStruct((4, 16, FF), LOW)
    in_vmem = pl.BlockSpec(memory_space=pltpu.VMEM)
    return pl.pallas_call(
        route_kernel,
        in_specs=[pl.BlockSpec(memory_space=pltpu.SMEM), in_vmem, in_vmem],
        out_specs=[in_vmem] * 4,
        out_shape=[half] * 4,
        scratch_shapes=[pltpu.VMEM((8, 32, FF), LOW)],
        compiler_params=pltpu.CompilerParams(vmem_limit_bytes=24 * 2**20),
        cost_estimate=pl.CostEstimate(flops=0, bytes_accessed=5 * 2**20, transcendentals=0),
    )(of, kept, got)


def shards(
    hidden_in,
    out_grad,
    seq_owner,
    token_place,
    matrix_slot,
    weight_slots,
    momentum_slots,
    gains,
    gain_momentum,
):
    slot_count, length = hidden_in.shape[:2]
    tok_count = slot_count * length
    z, y = lax.axis_index("dp_0"), lax.axis_index("dp_1")
    core, group = lax.axis_index("dp_2"), lax.axis_index("group")
    first_core = core == 0
    replica = ((z * 4 + y) * 2 + core) * 4 + group

    def core_pick(zero, one):
        return jnp.where(first_core, zero, one)

    weight_low = weight_slots.astype(LOW)
    (slots_top, slots_low), hidden_in = gather_group(
        [weight_low[:, :16], weight_low[:, 16:]], hidden_in
    )
    at = place_of(jnp.bitwise_xor(group, matrix_slot >> 1)) * 2 + (matrix_slot & 1)
    mine, theirs = compact(jnp.concatenate([at, core[None]]), slots_top, slots_low)
    got = swap(theirs)
    chip_rows = core_pick(
        jnp.concatenate([mine, got], axis=0), jnp.concatenate([got, mine], axis=0)
    )
    heads_held = gather_shaped(chip_rows[:, : 4 * HEADS_WIDTH], HEADS_WIDTH)
    inner_held = gather_shaped(chip_rows[:, 4 * HEADS_WIDTH :], INNER_WIDTH)
    column = lax.broadcasted_iota(jnp.int32, (D, D), 1)
    source = lax.broadcasted_iota(jnp.int32, (D, D), 0)
    block = column // 64
    near_z, near_y = block // 8, (block // 4) % 2
    far_z, far_y = (block // 2) % 2, block % 2
    from_z = jnp.bitwise_xor(z, jnp.bitwise_xor(near_z, far_z * 3))
    from_y = jnp.bitwise_xor(y, jnp.bitwise_xor(near_y, far_y * 3))
    reorder = (source == (from_z * 4 + from_y) * 64 + column % 64).astype(LOW)

    live_count = jnp.sum((seq_owner == replica).astype(jnp.int32))
    live_slot = (jnp.arange(slot_count, dtype=jnp.int32) < live_count).astype(F32)
    live_token = jnp.repeat(live_slot, length)[:, None]
    tokens = dot(hidden_in.reshape(tok_count, D), reorder)
    grad_out = dot(out_grad.reshape(tok_count, D), reorder) * live_token
    grad_low = both(grad_out.astype(LOW))
    layer_gains = jnp.dot(
        gains[: 2 * D].reshape(2, D), reorder.astype(F32), precision=lax.Precision.HIGHEST
    )
    gain_one, gain_two = layer_gains[0:1], layer_gains[1:2]
    gain_rows = jnp.pad(gains[2 * D :].reshape(2, HD), ((0, 6), (0, 0)))
    places = both(token_place).astype(F32).reshape(-1, 1)
    exponent = jnp.arange(HD // 2, dtype=F32) * (-2.0 / HD)
    angles = places * jnp.power(rope_base, exponent)[None, :]
    cosine, sine = jnp.cos(angles), jnp.sin(angles)
    cosine = jnp.concatenate([cosine, cosine], axis=1)
    sine = jnp.concatenate([-sine, sine], axis=1)

    scale_one = lax.rsqrt(jnp.mean(tokens * tokens, axis=-1, keepdims=True) + norm_eps)
    normed_one = tokens * scale_one
    input_one = both((normed_one * gain_one).astype(LOW))
    heads_held = together(gather_step(heads_held, 0))
    held = together([*gather_step(heads_held, 1), *gather_step(inner_held, 0)])
    held = together([*gather_step(held[:4], 2), *gather_step(held[4:], 1)])
    heads_held, inner_held = held[:4], held[4:]
    held = together([*gather_came(heads_held, 3), *gather_step(inner_held, 2)])
    w_heads = list(zip(heads_held, held[:4]))
    inner_held = held[4:]
    w_inner = [x for pair in zip(inner_held, gather_came(inner_held, 3)) for x in pair]
    raw, attn = [], []
    branch = jnp.zeros((2 * tok_count, D), F32)
    for i in range(4):
        fresh, heads, branch = heads_forward(
            (3 + i) % 4, input_one, w_heads[i], cosine, sine, gain_rows, branch
        )
        raw.append(fresh)
        attn.append(heads)
    *w_inner, branch = together([*w_inner, branch])
    residual = tokens + shared_sum(branch)
    scale_two = lax.rsqrt(jnp.mean(residual * residual, axis=-1, keepdims=True) + norm_eps)
    normed_two = residual * scale_two
    input_two = both((normed_two * gain_two).astype(LOW))
    act, grad_inner, outward, outward_other, grad_two, grad_two_other = inner_units(
        input_two, grad_low, w_inner
    )
    result = (residual + (outward + swap(outward_other).astype(F32))) * live_token
    hidden_out = dot(result.astype(LOW), reorder, LAST).astype(LOW)

    sent, kept = [], []
    for i in range(4):
        keep, send = terms(
            i, input_two, (grad_inner, i, FF // 4), grad_low, (act, i, FF // 8)
        )
        sent.append(send)
        kept.append(keep)
    grad_two = grad_two + swap(grad_two_other).astype(F32)
    gain_two_term = jnp.sum(grad_two * normed_two, axis=0, keepdims=True)
    grad_residual = grad_out + norm_back(grad_two * gain_two, normed_two, scale_two)
    branch_low = both(grad_residual.astype(LOW))
    grad_one, head_terms, grad_raw = jnp.zeros((2 * tok_count, D), F32), 0.0, []
    heads_sent, heads_kept = [], []

    def back_through(i, branch, grad_one):
        fresh, term, grad_one = heads_backward(
            (3 + i) % 4, raw[i], branch, w_heads[i], cosine, sine, gain_rows, grad_one
        )
        grad_raw.append(fresh)
        return head_terms + term, grad_one

    def heads_terms(i):
        keep, send = terms(
            i, input_one, (grad_raw[i], 0, 4 * HD), branch_low, (attn[i], 0, 2 * HD)
        )
        heads_kept.append(keep)
        heads_sent.append(send)

    head_terms, grad_one = back_through(0, branch_low, grad_one)
    head_terms, grad_one = back_through(1, branch_low, grad_one)
    sent, kept = scatter_step(sent, kept, 0)
    *held, branch_low, grad_one = together([*sent, *kept, branch_low, grad_one])
    sent, kept = held[:4], held[4:]
    head_terms, grad_one = back_through(2, branch_low, grad_one)
    heads_terms(0)
    sent, kept = scatter_step(sent, kept, 1)
    *held, branch_low, heads_sent[0], grad_one = together(
        [*sent, *kept, branch_low, heads_sent[0], grad_one]
    )
    sent, kept = held[:4], held[4:]
    head_terms, grad_one = back_through(3, branch_low, grad_one)
    heads_terms(1)
    sent, kept = scatter_step(sent, kept, 2)
    *held, heads_sent[1], grad_one = together([*sent, *kept, heads_sent[1], grad_one])
    sent, kept = held[:4], held[4:]
    heads_terms(2)
    heads_terms(3)
    sent, kept = scatter_step(sent, kept, 3)
    inner_sums = flat(kept)
    sent, kept = heads_sent, heads_kept
    grad_one = shared_sum(grad_one)
    gain_one_term = jnp.sum(grad_one * normed_one, axis=0, keepdims=True)
    in_grad = grad_residual + norm_back(grad_one * gain_one, normed_one, scale_one)
    in_high, in_low = split_two(in_grad)
    in_grad = dot(in_high, reorder, LAST) + dot(in_low, reorder, LAST)
    layer_terms = lax.dot_general(
        jnp.concatenate([gain_one_term, gain_two_term], axis=0),
        reorder.astype(F32),
        (LAST, ((), ())),
        precision=lax.Precision.HIGHEST,
    )
    gain_sum = jnp.concatenate([layer_terms.reshape(-1), head_terms[:2].reshape(-1)])
    for step in range(4):
        sent, kept = scatter_step(sent, kept, step)
        if step == 1:
            gain_sum = gain_sum + swap(gain_sum)
        elif step > 1:
            gain_sum = gain_sum + lax.ppermute(gain_sum, "group", (NEAR, FAR)[step - 2])
        if step == 0:
            *held, in_grad, gain_sum = together([*sent, *kept, in_grad, gain_sum])
        else:
            *held, gain_sum = together([*sent, *kept, gain_sum])
        sent, kept = held[:-4], held[-4:]
    heads_sums = flat(kept)

    sums = jnp.concatenate([*heads_sums, *inner_sums], axis=1)
    kept = core_pick(sums[:32], sums[32:])
    got = swap(core_pick(sums[32:], sums[:32]))
    slot_at = (jnp.bitwise_xor(group, jnp.asarray(MASKS, jnp.int32)) * 2)[:, None]
    slot_at = (slot_at + jnp.arange(2, dtype=jnp.int32)[None, :]).reshape(8)
    matches = slot_at[:, None] == matrix_slot[None, :]
    numbers = jnp.arange(7, dtype=jnp.int32)[None, :]
    routed_from = 7 - jnp.max(jnp.where(matches, 7 - numbers, 0), axis=1)
    halves = route(jnp.concatenate([routed_from, core[None]]), kept, got)
    sent, kept = [halves[1], halves[3]], [halves[0], halves[2]]
    for step in range(2):
        got = together(
            [lax.ppermute(sent[i], "group", (NEAR, FAR)[(step + i) % 2]) for i in range(2)]
        )
        total = [kept[i].astype(F32) + got[i].astype(F32) for i in range(2)]
        if step == 0:
            held = together([*(t[2:].astype(LOW) for t in total), *(t[:2].astype(LOW) for t in total)])
            sent, kept = held[:2], held[2:]
    weight_grad = jnp.concatenate(total, axis=1)

    own_ids = group * 2 + jnp.arange(2, dtype=jnp.int32)
    own_match = own_ids[:, None] == matrix_slot[None, :]
    own_width = jnp.sum(jnp.where(own_match, jnp.asarray(WIDTHS, jnp.int32)[None, :], 0), axis=1)
    own_width = own_width.astype(jnp.int32)
    column_mask = (jnp.arange(FF, dtype=jnp.int32)[None, :] < own_width[:, None]).astype(F32)
    column_mask = column_mask[:, None, :]
    momentum_new = column_mask * (momentum_keep * momentum_slots + weight_grad)
    direction = (weight_grad + momentum_keep * momentum_new).astype(LOW)

    mine = core_pick(direction[0], direction[1])
    got = swap(core_pick(direction[1], direction[0]))
    rows = core_pick(jnp.concatenate([mine, got], axis=0), jnp.concatenate([got, mine], axis=0))
    gain_parts, rest = [], gain_sum
    for _ in range(3):
        part = lax.reduce_precision(rest, exponent_bits=8, mantissa_bits=7)
        gain_parts.append(part.astype(LOW))
        rest = rest - part
    gain_parts = jnp.pad(jnp.concatenate(gain_parts), (0, 64 * HD - 3 * gain_sum.shape[0]))
    held = gather_shaped(rows, FF // 4)
    held[0] = jnp.concatenate([held[0], gain_parts.reshape(1, 1, 1, 1, 64, HD)], axis=-1)
    for step in range(3):
        held = together(gather_step(held, step))
    fresh = gather_came(held, 3)
    pieces = [x for pair in zip(held, fresh) for x in pair]
    gain_parts = [x[..., FF // 4 :] for x in pieces[:2]]
    *gain_parts, iterate = together([*gain_parts, iterate_rows(pieces)])
    gain_parts = jnp.concatenate(gain_parts, axis=3)
    gain_parts = gain_parts.reshape(16, 64 * HD)
    place = lax.broadcasted_iota(jnp.int32, (16, 16), 1)
    of_z = jnp.bitwise_xor(z, jnp.bitwise_xor(place // 8, (place // 2) % 2 * 3))
    of_y = jnp.bitwise_xor(y, jnp.bitwise_xor((place // 4) % 2, place % 2 * 3))
    in_turn = (lax.broadcasted_iota(jnp.int32, (16, 16), 0) == of_z * 4 + of_y).astype(LOW)
    gain_parts = dot(in_turn, gain_parts)[:, : 3 * gain_sum.shape[0]].reshape(16, 3, -1)
    gain_grad = jnp.sum(gain_parts[:, 0] + gain_parts[:, 1] + gain_parts[:, 2], axis=0)
    kept = core_pick(iterate[:32], iterate[32:])
    got = swap(core_pick(iterate[32:], iterate[:32]))
    iterate = jnp.stack([core_pick(kept, got), core_pick(got, kept)]).astype(F32)
    update_scale = 0.2 * jnp.sqrt(jnp.maximum(own_width, D).astype(F32))
    weight_new = column_mask * (
        weight_slots * (1.0 - learn_rate * weight_decay)
        - learn_rate * update_scale[:, None, None] * iterate
    )

    gain_momentum_new = momentum_keep * gain_momentum + gain_grad
    gain_step = gain_grad + momentum_keep * gain_momentum_new
    rows = gain_step.reshape(18, HD)
    part = jnp.minimum(jnp.arange(18) // 8, 1) + (jnp.arange(18) // 16) * (jnp.arange(18) - 15)
    alike = part[:, None] == part[None, :]
    squares = jnp.sum(rows * rows, axis=1)
    sums = jnp.sum(jnp.where(alike, squares[None, :], 0.0), axis=1, keepdims=True)
    counts = jnp.sum(jnp.where(alike, float(HD), 0.0), axis=1, keepdims=True)
    scaled = rows * lax.rsqrt(sums / counts + norm_eps)
    gain_new = gains - gain_rate * scaled.reshape(-1)
    shape = (slot_count, length, D)
    return (
        hidden_out.reshape(shape),
        in_grad.reshape(shape),
        weight_grad,
        momentum_new,
        weight_new,
        gain_grad,
        gain_momentum_new,
        gain_new,
    )


def solution(mesh):
    finer = Mesh(
        mesh.devices.reshape(4, 4, 2, mesh.shape["group"]), ("dp_0", "dp_1", "dp_2", "group")
    )
    in_specs = (
        P(DP_GROUP, None, None),
        P(DP_GROUP, None, None),
        P(),
        P(DP_GROUP, None),
        P(),
        P("group", ("dp_0", "dp_1", "dp_2"), None),
        P("group", ("dp_0", "dp_1", "dp_2"), None),
        P(),
        P(),
    )
    out_specs = (
        P(DP_GROUP, None, None),
        P(DP_GROUP, None, None),
        P("group", ("dp_0", "dp_1", "dp_2"), None),
        P("group", ("dp_0", "dp_1", "dp_2"), None),
        P("group", ("dp_0", "dp_1", "dp_2"), None),
        P(),
        P(),
        P(),
    )
    return jax.shard_map(
        shards, mesh=finer, in_specs=in_specs, out_specs=out_specs, check_vma=False
    )
```
